256 devices in a mesh: grp: 2 (over core), ep: 128 (over x, y, z).
Axes of the slice: x: 4, y: 4, z: 8, core: 2. Of those that a mesh axis runs over, the one named last changes fastest.
Arguments:
- tokens: float32 [4096, 6144], P('ep'), may hold values from -6 to 6
- route_ids: int32 [4096, 12], P('ep'), may hold values from 0 to 767, as said below
- route_weights: float32 [4096, 12], P('ep'), may hold values from 0.05 to 1
- expert_rows: float32 [512, 96, 6144], P(('grp', 'ep')), may hold values from -6 to 6
Outputs:
- combined: float32 [4096, 6144], P('ep', 'grp')
The draws below stay inside these ranges and needn't reach their ends.
Inputs may be any that keep to these rules, and one draw needn't show every extreme that they name: `route_ids`: each row names 12 different experts. Each routed expert is chosen by at most 96 tokens in all, and by at most 1 of the 32 tokens of one ep index; some routed expert reaches each of these bounds in every draw. Values 512 and above are identity experts.
All inputs are finite; a program needn't handle non-finite values.
Results may differ from the reference program's by a relative error of at most 0.00002.
Values sent between devices are 32-bit elements; how exact they have to be, the bound alone decides.
No kernel may reach another device: no remote copies, remote signals or barrier semaphores. Data moves between devices by JAX's collectives and lax.ppermute only.
A program may use at most 64 MiB of HBM per device.

```python
import math
import jax
import jax.numpy as jnp
import numpy as np

D = 6144
TOP = 12
TOK_DEV = 32
TOKENS = 4096
EXPERTS = 512
ZEXP = 256
LANE = 64
CAP = 96
N_GRP = 2


def quota_table():
    rest = TOKENS - CAP - CAP // 2
    base = rest // (LANE - 2)
    extra = rest % (LANE - 2)
    table = [CAP, CAP // 2] + [base + (1 if j < extra else 0) for j in range(LANE - 2)]
    return np.array(table, dtype=np.int32)


def draw_route_ids(key, part):
    key = jax.random.fold_in(key, 7311)
    homes = TOKENS // TOK_DEV
    quotas = jnp.asarray(quota_table())
    values = jnp.repeat(jnp.arange(LANE, dtype=jnp.int32), quotas, total_repeat_length=TOKENS)
    key_real, key_rest, key_lanes = jax.random.split(key, 3)
    real_order = jax.random.permutation(key_real, EXPERTS).astype(jnp.int32)
    others = jnp.concatenate([real_order[TOP:], EXPERTS + jnp.arange(ZEXP, dtype=jnp.int32)])
    others = jax.random.permutation(key_rest, others).astype(jnp.int32)
    labels = jnp.concatenate([real_order[:TOP][:, None], others.reshape(TOP, LANE - 1)], axis=1)
    columns = []
    lane_keys = jax.random.split(key_lanes, TOP)
    for lane in range(TOP):
        key_shift, key_pos = jax.random.split(lane_keys[lane])
        layout = values.reshape(TOK_DEV, homes).T
        shift = jax.random.randint(key_shift, (), 0, homes)
        layout = jnp.roll(layout, shift, axis=0)
        pos_keys = jax.random.split(key_pos, homes)
        orders = jax.vmap(lambda k: jax.random.permutation(k, TOK_DEV))(pos_keys)
        layout = jnp.take_along_axis(layout, orders.astype(jnp.int32), axis=1)
        picks = layout.reshape(TOKENS)
        columns.append(labels[lane][picks])
    return jnp.stack(columns, axis=1).astype(jnp.int32)


def levels(key, dims, shards, least, largest):
    factor_of, own = 1.0, jax.random.fold_in(key, 6)
    for position, shards_of in shards:
        steps = jnp.exp(jax.random.uniform(jax.random.fold_in(own, position), (shards_of,), jnp.float32, least / len(shards), largest / len(shards)))
        factor_of = factor_of * jnp.repeat(steps, dims[position] // shards_of).reshape([-1 if axis == position else 1 for axis in range(len(dims))])
    return factor_of


def bell_draw(rng, dims, scale, bound, pieces=(), kind=jnp.bfloat16):
    level = levels(rng, dims, pieces, -0.22, 0.18) if pieces else 1.0
    result = jax.random.normal(rng, dims, jnp.float32) * scale * level
    return jnp.minimum(jnp.maximum(result, -bound), bound).astype(kind)


def setup_inputs(seed: int = 0) -> dict:
    key_list = jax.random.split(jax.random.key(seed), 5)
    return {
        "tokens": bell_draw(key_list[0], (TOKENS, D), 1.0, 6.0, ((0, 128),), jnp.float32),
        "route_ids": draw_route_ids(jax.random.fold_in(key_list[4], 71), 0),
        "route_weights": jnp.clip(jnp.exp(math.log(1.0) - 2.9957323 * jax.random.uniform(key_list[2], (TOKENS, TOP), jnp.float32) ** levels(key_list[2], (TOKENS, TOP), ((0, 128),), -0.2, 0.2)), 0.05, 1.0),
        "expert_rows": bell_draw(key_list[3], (EXPERTS, CAP, D), 1.0, 6.0, ((0, 256),), jnp.float32),
    }


def reference(tokens, route_ids, route_weights, expert_rows):
    real = route_ids < EXPERTS
    group = jnp.where(real, route_ids // (EXPERTS // N_GRP), (route_ids - EXPERTS) // (ZEXP // N_GRP))
    chosen = (route_ids[:, :, None] == jnp.arange(EXPERTS, dtype=jnp.int32)[None, None, :]).astype(jnp.int32).sum(1)
    before = jnp.cumsum(chosen, axis=0) - chosen
    safe_expert = jnp.where(real, route_ids, 0).astype(jnp.int32)
    rank = jnp.take_along_axis(before, safe_expert, axis=1)
    safe_rank = jnp.where(real, rank, 0).astype(jnp.int32)
    partials = []
    for which in range(N_GRP):
        total = jnp.zeros((TOKENS, D), jnp.float32)
        for slot in range(TOP):
            rows = expert_rows[safe_expert[:, slot], safe_rank[:, slot]]
            value = jnp.where(real[:, slot][:, None], rows, tokens)
            factor = jnp.where(group[:, slot] == which, route_weights[:, slot], jnp.zeros_like(route_weights[:, slot]))
            total = total + factor[:, None] * value
        partials.append(total)
    combined = partials[0]
    for which in range(1, N_GRP):
        combined = combined + partials[which]
    return combined
```

```python
import jax
import jax.numpy as jnp
from jax import lax
from jax.sharding import Mesh
from jax.sharding import PartitionSpec as P

EP = ("x", "y", "zh", "zl")
NEAR = ("x", "y", "zl")
EXACT = lax.Precision.HIGHEST


def shards(tokens, route_ids, route_weights, expert_rows):
    group = lax.axis_index("grp")
    ep_count = lax.axis_size(EP)
    far = lax.axis_size("zh")
    low = lax.axis_size("zl")
    near = ep_count // far
    tok_dev, top = route_ids.shape
    exp_dev, capacity, width = expert_rows.shape
    half = width // 2
    held = 2 * exp_dev
    per_group = exp_dev * ep_count
    experts = 2 * per_group

    own = lax.dynamic_slice_in_dim(expert_rows, group * half, half, 2)
    given = lax.dynamic_slice_in_dim(expert_rows, (1 - group) * half, half, 2)
    taken = lax.ppermute(given, "grp", [(0, 1), (1, 0)])
    table = jnp.concatenate([own, taken], axis=0).reshape(held * capacity, half)

    real = route_ids < experts
    ids_t = route_ids.T
    chip = jnp.where(ids_t < experts, ids_t % per_group // exp_dev, -1)
    place = (ids_t // per_group != group) * exp_dev + ids_t % exp_dev
    lanes = jnp.arange(128, dtype=jnp.int32)
    chip_hot = (chip[:, :, None] == jnp.arange(ep_count, dtype=jnp.int32)).astype(jnp.bfloat16)
    place_hot = (place[:, :, None] == lanes).astype(jnp.bfloat16)
    flags = lax.dot_general(
        chip_hot.reshape(top * tok_dev, ep_count), place_hot.reshape(top * tok_dev, 128),
        (((0,), (0,)), ((), ())), preferred_element_type=jnp.float32,
    )
    chosen = lax.all_to_all(flags[:, None, :], EP, 0, 0, tiled=True).reshape(ep_count, 128)
    chosen = chosen.astype(jnp.bfloat16)

    row = jnp.arange(ep_count * held, dtype=jnp.int32)[:, None]
    r_exp = row % held
    r_far = row // held % far
    r_near = row // (held * far)
    home = (r_near // low * far + r_far) * low + r_near % low
    homes = jnp.arange(ep_count, dtype=jnp.int32)[None, :]
    before = jnp.dot((homes < home).astype(jnp.bfloat16), chosen, preferred_element_type=jnp.float32)
    here = jnp.dot((homes == home).astype(jnp.bfloat16), chosen, preferred_element_type=jnp.float32)
    mine = lanes[None, :] == r_exp
    rank = jnp.sum(jnp.where(mine, before, 0.0), axis=1, keepdims=True)
    hit = jnp.sum(jnp.where(mine, here, 0.0), axis=1, keepdims=True)
    code = jnp.where(hit > 0, rank.astype(jnp.int32) + capacity * r_exp, -1)
    select = (code == jnp.arange(held * capacity, dtype=jnp.int32)[None, :]).astype(jnp.float32)
    outgoing = jnp.dot(select, table, precision=EXACT).reshape(near, far * held, half)

    rows = lax.all_to_all(outgoing, NEAR, 0, 0, tiled=True).reshape(ep_count * held, half)

    pair = jnp.concatenate([route_ids.astype(jnp.float32), route_weights], axis=1)
    pairs = lax.all_gather(pair, "zh", axis=0, tiled=True)
    col = jnp.arange(ep_count * held, dtype=jnp.int32)[None, :]
    c_exp = col % held
    c_far = col // held % far
    c_near = col // (held * far)
    c_chip = (c_near // low * far + lax.axis_index("zh")) * low + c_near % low
    c_group = jnp.where(c_exp < exp_dev, group, 1 - group)
    c_id = (c_group * per_group + c_chip * exp_dev + c_exp % exp_dev).astype(jnp.float32)
    mix = jnp.zeros((far * tok_dev, ep_count * held), jnp.float32)
    for k in range(top):
        mix = mix + jnp.where(pairs[:, k : k + 1] == c_id, pairs[:, top + k : top + k + 1], 0.0)
    line = jnp.arange(far * tok_dev, dtype=jnp.int32)[:, None]
    mix = jnp.where(line // tok_dev == c_far, mix, 0.0)
    partial = jnp.dot(mix, rows, precision=EXACT).reshape(far, tok_dev, half)
    total = lax.psum_scatter(partial, "zh", scatter_dimension=0, tiled=True).reshape(tok_dev, half)

    ident = jnp.sum(jnp.where(real, 0.0, route_weights), axis=1, keepdims=True)
    return total + ident * lax.dynamic_slice_in_dim(tokens, group * half, half, 1)


def solution(mesh):
    torus = Mesh(mesh.devices.reshape(mesh.shape["grp"], 4, 4, 4, 2), ("grp",) + EP)
    in_specs = (P(EP, None), P(EP, None), P(EP, None), P(("grp",) + EP, None, None))
    return jax.shard_map(
        shards, mesh=torus, in_specs=in_specs, out_specs=P(EP, "grp"), check_vma=False
    )
```

```python
import jax
import jax.numpy as jnp
from jax import lax
from jax.sharding import Mesh
from jax.sharding import PartitionSpec as P

EP = ("x", "y", "zh", "zl")
NEAR = ("x", "y", "zl")
EXACT = lax.Precision.HIGHEST


def shift(count, by):
    return [(i, (i + by) % count) for i in range(count)]


def shards(tokens, route_ids, route_weights, expert_rows):
    group = lax.axis_index("grp")
    ep_count = lax.axis_size(EP)
    far = lax.axis_size("zh")
    low = lax.axis_size("zl")
    near = ep_count // far
    tok_dev, top = route_ids.shape
    exp_dev, capacity, width = expert_rows.shape
    half = width // 2
    held = 2 * exp_dev
    per_group = exp_dev * ep_count
    experts = 2 * per_group

    own = lax.dynamic_slice_in_dim(expert_rows, group * half, half, 2)
    given = lax.dynamic_slice_in_dim(expert_rows, (1 - group) * half, half, 2)
    taken = lax.ppermute(given, "grp", [(0, 1), (1, 0)])
    table = jnp.concatenate([own, taken], axis=0).reshape(held * capacity, half)

    real = route_ids < experts
    ids_t = route_ids.T
    chip = jnp.where(ids_t < experts, ids_t % per_group // exp_dev, -1)
    place = (ids_t // per_group != group) * exp_dev + ids_t % exp_dev
    lanes = jnp.arange(128, dtype=jnp.int32)
    chip_hot = (chip[:, :, None] == jnp.arange(ep_count, dtype=jnp.int32)).astype(jnp.bfloat16)
    place_hot = (place[:, :, None] == lanes).astype(jnp.bfloat16)
    flags = lax.dot_general(
        chip_hot.reshape(top * tok_dev, ep_count), place_hot.reshape(top * tok_dev, 128),
        (((0,), (0,)), ((), ())), preferred_element_type=jnp.float32,
    )
    chosen = lax.all_to_all(flags[:, None, :], EP, 0, 0, tiled=True).reshape(ep_count, 128)
    chosen = chosen.astype(jnp.bfloat16)

    row = jnp.arange(ep_count * held, dtype=jnp.int32)[:, None]
    r_exp = row % held
    r_far = row // held % far
    r_near = row // (held * far)
    r_home = (lax.axis_index("zh") + r_far) % far
    home = (r_near // low * far + r_home) * low + r_near % low
    homes = jnp.arange(ep_count, dtype=jnp.int32)[None, :]
    before = jnp.dot((homes < home).astype(jnp.bfloat16), chosen, preferred_element_type=jnp.float32)
    here = jnp.dot((homes == home).astype(jnp.bfloat16), chosen, preferred_element_type=jnp.float32)
    mine = lanes[None, :] == r_exp
    rank = jnp.sum(jnp.where(mine, before, 0.0), axis=1, keepdims=True)
    hit = jnp.sum(jnp.where(mine, here, 0.0), axis=1, keepdims=True)
    code = jnp.where(hit > 0, rank.astype(jnp.int32) + capacity * r_exp, -1)
    select = (code == jnp.arange(held * capacity, dtype=jnp.int32)[None, :]).astype(jnp.float32)
    outgoing = jnp.dot(select, table, precision=EXACT).reshape(near, far * held, half)

    rows = lax.all_to_all(outgoing, NEAR, 0, 0, tiled=True).reshape(ep_count * held, half)

    pair = jnp.concatenate([route_ids.astype(jnp.float32), route_weights], axis=1)
    pairs = jnp.concatenate(
        [pair] + [lax.ppermute(pair, "zh", shift(far, -o)) for o in range(1, far)], axis=0
    )
    col = jnp.arange(ep_count * held, dtype=jnp.int32)[None, :]
    c_exp = col % held
    c_far = col // held % far
    c_near = col // (held * far)
    c_chip = (c_near // low * far + lax.axis_index("zh")) * low + c_near % low
    c_group = jnp.where(c_exp < exp_dev, group, 1 - group)
    c_id = (c_group * per_group + c_chip * exp_dev + c_exp % exp_dev).astype(jnp.float32)
    mix = jnp.zeros((far * tok_dev, ep_count * held), jnp.float32)
    for k in range(top):
        mix = mix + jnp.where(pairs[:, k : k + 1] == c_id, pairs[:, top + k : top + k + 1], 0.0)
    line = jnp.arange(far * tok_dev, dtype=jnp.int32)[:, None]
    mix = jnp.where(line // tok_dev == c_far, mix, 0.0)
    partial = jnp.dot(mix, rows, precision=EXACT).reshape(far, tok_dev, half)
    cut = half // 2
    up, down = shift(far, 1), shift(far, -1)
    far_up = lax.ppermute(partial[2, :, :cut], "zh", up)
    far_down = lax.ppermute(partial[2, :, cut:], "zh", down)
    next_right = lax.ppermute(partial[1, :, cut:], "zh", up)
    prev_left = lax.ppermute(partial[3, :, :cut], "zh", down)
    next_left = lax.ppermute(partial[1, :, :cut] + far_up, "zh", up)
    prev_right = lax.ppermute(partial[3, :, cut:] + far_down, "zh", down)
    total = partial[0] + jnp.concatenate([next_left + prev_left, next_right + prev_right], axis=1)

    ident = jnp.sum(jnp.where(real, 0.0, route_weights), axis=1, keepdims=True)
    return total + ident * lax.dynamic_slice_in_dim(tokens, group * half, half, 1)


def solution(mesh):
    torus = Mesh(mesh.devices.reshape(mesh.shape["grp"], 4, 4, 4, 2), ("grp",) + EP)
    in_specs = (P(EP, None), P(EP, None), P(EP, None), P(("grp",) + EP, None, None))
    return jax.shard_map(
        shards, mesh=torus, in_specs=in_specs, out_specs=P(EP, "grp"), check_vma=False
    )
```

```python
import jax
import jax.numpy as jnp
from jax import lax
from jax.sharding import Mesh
from jax.sharding import PartitionSpec as P
from jax.experimental import pallas as pl
from jax.experimental.pallas import tpu as pltpu

EP = ("x", "y", "zh", "zl")
NEAR = ("x", "y", "zl")
BLOCK = 512
VMEM = 40 * 1024 * 1024


def thirds(x):
    high = x.astype(jnp.bfloat16)
    rest = x - high.astype(jnp.float32)
    middle = rest.astype(jnp.bfloat16)
    low = (rest - middle.astype(jnp.float32)).astype(jnp.bfloat16)
    return high, middle, low


def mul(a, b):
    return jnp.dot(a, b, preferred_element_type=jnp.float32)


def pick_kernel(group_ref, code_ref, own_ref, taken_ref, out_ref, select):
    @pl.when(pl.program_id(0) == 0)
    def _():
        slot = lax.broadcasted_iota(jnp.int32, select.shape, 1)
        select[...] = (code_ref[...] == slot).astype(jnp.float32).astype(jnp.bfloat16)

    flat = (own_ref.shape[0] * own_ref.shape[1], own_ref.shape[2])
    table = jnp.concatenate([own_ref[...].reshape(flat), taken_ref[...].reshape(flat)], axis=0)
    high, middle, low = thirds(table)
    chosen = select[...]
    out_ref[...] = mul(chosen, high) + mul(chosen, middle) + mul(chosen, low)


def pick(group, code, expert_rows, taken):
    exp_dev, capacity, half = taken.shape
    steps = half // BLOCK
    count = code.shape[0]
    slots = 2 * exp_dev * capacity
    block = (exp_dev, capacity, BLOCK)
    return pl.pallas_call(
        pick_kernel,
        out_shape=jax.ShapeDtypeStruct((count, half), jnp.float32),
        grid_spec=pltpu.PrefetchScalarGridSpec(
            num_scalar_prefetch=1,
            grid=(steps,),
            in_specs=[
                pl.BlockSpec((count, 1), lambda i, g: (0, 0)),
                pl.BlockSpec(block, lambda i, g: (0, 0, g[0] * steps + i)),
                pl.BlockSpec(block, lambda i, g: (0, 0, i)),
            ],
            out_specs=pl.BlockSpec((count, BLOCK), lambda i, g: (0, i)),
            scratch_shapes=[pltpu.VMEM((count, slots), jnp.bfloat16)],
        ),
        compiler_params=pltpu.CompilerParams(vmem_limit_bytes=VMEM),
        cost_estimate=pl.CostEstimate(
            flops=6 * count * slots * half, bytes_accessed=4 * (slots + count) * half, transcendentals=0
        ),
        name="pick",
    )(group, code, expert_rows, taken)


def combine_kernel(mix_ref, rows_ref, out_ref):
    m_high, m_middle, m_low = thirds(mix_ref[...])
    r_high, r_middle, r_low = thirds(rows_ref[...])
    small = mul(m_low, r_high) + mul(m_middle, r_middle) + mul(m_high, r_low)
    small += mul(m_middle, r_high) + mul(m_high, r_middle)
    out_ref[...] = small + mul(m_high, r_high)


def combine(mix, rows):
    count, depth = mix.shape
    half = rows.shape[1]
    return pl.pallas_call(
        combine_kernel,
        out_shape=jax.ShapeDtypeStruct((count, half), jnp.float32),
        grid=(half // BLOCK,),
        in_specs=[
            pl.BlockSpec((count, depth), lambda i: (0, 0)),
            pl.BlockSpec((depth, BLOCK), lambda i: (0, i)),
        ],
        out_specs=pl.BlockSpec((count, BLOCK), lambda i: (0, i)),
        compiler_params=pltpu.CompilerParams(vmem_limit_bytes=VMEM),
        cost_estimate=pl.CostEstimate(
            flops=12 * count * depth * half, bytes_accessed=4 * (count + depth) * half, transcendentals=0
        ),
        name="combine",
    )(mix, rows)


def shift(count, by):
    return [(i, (i + by) % count) for i in range(count)]


def shards(tokens, route_ids, route_weights, expert_rows):
    group = lax.axis_index("grp")
    ep_count = lax.axis_size(EP)
    far = lax.axis_size("zh")
    low = lax.axis_size("zl")
    near = ep_count // far
    tok_dev, top = route_ids.shape
    exp_dev, capacity, width = expert_rows.shape
    half = width // 2
    held = 2 * exp_dev
    per_group = exp_dev * ep_count
    experts = 2 * per_group

    given = lax.dynamic_slice_in_dim(expert_rows, (1 - group) * half, half, 2)
    taken = lax.ppermute(given, "grp", [(0, 1), (1, 0)])

    real = route_ids < experts
    ids_t = route_ids.T
    chip = jnp.where(ids_t < experts, ids_t % per_group // exp_dev, -1)
    place = (ids_t // per_group != group) * exp_dev + ids_t % exp_dev
    lanes = jnp.arange(128, dtype=jnp.int32)
    chip_hot = (chip[:, :, None] == jnp.arange(ep_count, dtype=jnp.int32)).astype(jnp.bfloat16)
    place_hot = (place[:, :, None] == lanes).astype(jnp.bfloat16)
    flags = lax.dot_general(
        chip_hot.reshape(top * tok_dev, ep_count), place_hot.reshape(top * tok_dev, 128),
        (((0,), (0,)), ((), ())), preferred_element_type=jnp.float32,
    )
    chosen = lax.all_to_all(flags[:, None, :], EP, 0, 0, tiled=True).reshape(ep_count, 128)
    pair = jnp.concatenate([route_ids.astype(jnp.float32), route_weights], axis=1)
    pairs = jnp.concatenate(
        [pair] + [lax.ppermute(pair, "zh", shift(far, -o)) for o in range(1, far)], axis=0
    )
    chosen, pairs = lax.optimization_barrier((chosen.astype(jnp.bfloat16), pairs))

    row = jnp.arange(ep_count * held, dtype=jnp.int32)[:, None]
    r_exp = row % held
    r_far = row // held % far
    r_near = row // (held * far)
    r_home = (lax.axis_index("zh") + r_far) % far
    home = (r_near // low * far + r_home) * low + r_near % low
    homes = jnp.arange(ep_count, dtype=jnp.int32)[None, :]
    before = jnp.dot((homes < home).astype(jnp.bfloat16), chosen, preferred_element_type=jnp.float32)
    here = jnp.dot((homes == home).astype(jnp.bfloat16), chosen, preferred_element_type=jnp.float32)
    mine = lanes[None, :] == r_exp
    rank = jnp.sum(jnp.where(mine, before, 0.0), axis=1, keepdims=True)
    hit = jnp.sum(jnp.where(mine, here, 0.0), axis=1, keepdims=True)
    code = jnp.where(hit > 0, rank.astype(jnp.int32) + capacity * r_exp, -1)
    outgoing = pick(group.astype(jnp.int32).reshape(1), code, expert_rows, taken)
    outgoing = outgoing.reshape(near, far * held, half)

    rows = lax.all_to_all(outgoing, NEAR, 0, 0, tiled=True).reshape(ep_count * held, half)

    col = jnp.arange(ep_count * held, dtype=jnp.int32)[None, :]
    c_exp = col % held
    c_far = col // held % far
    c_near = col // (held * far)
    c_chip = (c_near // low * far + lax.axis_index("zh")) * low + c_near % low
    c_group = jnp.where(c_exp < exp_dev, group, 1 - group)
    c_id = (c_group * per_group + c_chip * exp_dev + c_exp % exp_dev).astype(jnp.float32)
    mix = jnp.zeros((far * tok_dev, ep_count * held), jnp.float32)
    for k in range(top):
        mix = mix + jnp.where(pairs[:, k : k + 1] == c_id, pairs[:, top + k : top + k + 1], 0.0)
    line = jnp.arange(far * tok_dev, dtype=jnp.int32)[:, None]
    mix = jnp.where(line // tok_dev == c_far, mix, 0.0)
    partial = combine(mix, rows).reshape(far, tok_dev, half)
    cut = half // 2
    up, down = shift(far, 1), shift(far, -1)
    far_up = lax.ppermute(partial[2, :, :cut], "zh", up)
    far_down = lax.ppermute(partial[2, :, cut:], "zh", down)
    next_right = lax.ppermute(partial[1, :, cut:], "zh", up)
    prev_left = lax.ppermute(partial[3, :, :cut], "zh", down)
    next_left = lax.ppermute(partial[1, :, :cut] + far_up, "zh", up)
    prev_right = lax.ppermute(partial[3, :, cut:] + far_down, "zh", down)
    total = partial[0] + jnp.concatenate([next_left + prev_left, next_right + prev_right], axis=1)

    ident = jnp.sum(jnp.where(real, 0.0, route_weights), axis=1, keepdims=True)
    return total + ident * lax.dynamic_slice_in_dim(tokens, group * half, half, 1)


def solution(mesh):
    torus = Mesh(mesh.devices.reshape(mesh.shape["grp"], 4, 4, 4, 2), ("grp",) + EP)
    in_specs = (P(EP, None), P(EP, None), P(EP, None), P(("grp",) + EP, None, None))
    return jax.shard_map(
        shards, mesh=torus, in_specs=in_specs, out_specs=P(EP, "grp"), check_vma=False
    )
```

```python
import jax
import jax.numpy as jnp
from jax import lax
from jax.sharding import Mesh
from jax.sharding import PartitionSpec as P
from jax.experimental import pallas as pl
from jax.experimental.pallas import tpu as pltpu

EP = ("x", "y", "zh", "zl")
NEAR = ("x", "y", "zl")
BLOCK = 512
PICK_VMEM = 20 * 1024 * 1024
MIX_VMEM = 16 * 1024 * 1024


def halves(x):
    high = x.astype(jnp.bfloat16)
    rest = x - high.astype(jnp.float32)
    middle = rest.astype(jnp.bfloat16)
    return high, middle, rest - middle.astype(jnp.float32)


def mul(a, b):
    return jnp.dot(a, b, preferred_element_type=jnp.float32)


def pick_kernel(group_ref, code_ref, own_ref, taken_ref, out_ref, select):
    @pl.when(pl.program_id(0) == 0)
    def _():
        slot = lax.broadcasted_iota(jnp.int32, select.shape, 1)
        select[...] = (code_ref[...] == slot).astype(jnp.float32).astype(jnp.bfloat16)

    targets, rows, columns = out_ref.shape
    each = targets * rows // 2
    for part, ref in enumerate((own_ref, taken_ref)):
        table = ref[...].reshape(ref.shape[0] * ref.shape[1], columns)
        high, middle, rest = halves(table)
        chosen = select[part * each : (part + 1) * each, :]
        value = mul(chosen, high) + mul(chosen, middle) + mul(chosen, rest.astype(jnp.bfloat16))
        out_ref[:, part * rows // 2 : (part + 1) * rows // 2, :] = value.reshape(targets, rows // 2, columns)


def pick(group, code, own, taken, targets):
    exp_dev, capacity, width = own.shape
    half = width // 2
    steps = half // BLOCK
    count = code.shape[0]
    slots = exp_dev * capacity
    block = pl.BlockSpec((exp_dev, capacity, BLOCK), lambda i, g: (0, 0, g[0] * steps + i))
    return pl.pallas_call(
        pick_kernel,
        out_shape=jax.ShapeDtypeStruct((targets, count // targets, half), jnp.float32),
        grid_spec=pltpu.PrefetchScalarGridSpec(
            num_scalar_prefetch=1,
            grid=(steps,),
            in_specs=[pl.BlockSpec((count, 1), lambda i, g: (0, 0)), block, block],
            out_specs=pl.BlockSpec((targets, count // targets, BLOCK), lambda i, g: (0, 0, i)),
            scratch_shapes=[pltpu.VMEM((count, slots), jnp.bfloat16)],
        ),
        compiler_params=pltpu.CompilerParams(vmem_limit_bytes=PICK_VMEM),
        cost_estimate=pl.CostEstimate(
            flops=6 * count * slots * half, bytes_accessed=4 * (2 * slots + count) * half, transcendentals=0
        ),
        name="pick",
    )(group, code, own, taken)


def combine_kernel(pairs_ref, ids_ref, rows_ref, out_ref, mix):
    count = mix.shape[0] // 2

    @pl.when(pl.program_id(0) == 0)
    def _():
        pairs = pairs_ref[...].T
        top = pairs.shape[1] // 2
        ids = ids_ref[0:1, :]
        total = jnp.zeros((count, mix.shape[1]), jnp.float32)
        for k in range(top):
            total += jnp.where(pairs[:, k : k + 1] == ids, pairs[:, top + k : top + k + 1], 0.0)
        line = lax.broadcasted_iota(jnp.int32, total.shape, 0) * 4 // count
        total = jnp.where(line.astype(jnp.float32) == ids_ref[1:2, :], total, 0.0)
        high, middle, _ = halves(total)
        mix[:count, :] = high
        mix[count:, :] = middle

    high, middle, _ = halves(rows_ref[...])
    both = mul(mix[...], high)
    out_ref[...] = both[:count] + (both[count:] + mul(mix[:count, :], middle))


def combine(pairs, ids, rows):
    count = pairs.shape[1]
    depth, half = rows.shape
    return pl.pallas_call(
        combine_kernel,
        out_shape=jax.ShapeDtypeStruct((count, half), jnp.float32),
        grid=(half // BLOCK,),
        in_specs=[
            pl.BlockSpec(pairs.shape, lambda i: (0, 0)),
            pl.BlockSpec(ids.shape, lambda i: (0, 0)),
            pl.BlockSpec((depth, BLOCK), lambda i: (0, i)),
        ],
        out_specs=pl.BlockSpec((count, BLOCK), lambda i: (0, i)),
        scratch_shapes=[pltpu.VMEM((2 * count, depth), jnp.bfloat16)],
        compiler_params=pltpu.CompilerParams(vmem_limit_bytes=MIX_VMEM),
        cost_estimate=pl.CostEstimate(
            flops=6 * count * depth * half, bytes_accessed=4 * (count + depth) * half, transcendentals=0
        ),
        name="combine",
    )(pairs, ids, rows)


def shift(count, by):
    return [(i, (i + by) % count) for i in range(count)]


def shards(tokens, route_ids, route_weights, expert_rows):
    group = lax.axis_index("grp")
    ep_count = lax.axis_size(EP)
    far = lax.axis_size("zh")
    low = lax.axis_size("zl")
    near = ep_count // far
    tok_dev, top = route_ids.shape
    exp_dev, capacity, width = expert_rows.shape
    half = width // 2
    held = 2 * exp_dev
    per_group = exp_dev * ep_count
    experts = 2 * per_group

    taken = lax.ppermute(expert_rows, "grp", [(0, 1), (1, 0)])

    ids_t = route_ids.T
    chip = jnp.where(ids_t < experts, ids_t % per_group // exp_dev, -1)
    place = (ids_t // per_group != group) * exp_dev + ids_t % exp_dev
    lanes = jnp.arange(128, dtype=jnp.int32)
    chip_hot = (chip[:, :, None] == jnp.arange(ep_count, dtype=jnp.int32)).astype(jnp.bfloat16)
    place_hot = (place[:, :, None] == lanes).astype(jnp.bfloat16)
    flags = lax.dot_general(
        chip_hot.reshape(top * tok_dev, ep_count), place_hot.reshape(top * tok_dev, 128),
        (((0,), (0,)), ((), ())), preferred_element_type=jnp.float32,
    )
    chosen = lax.all_to_all(flags[:, None, :], EP, 0, 0, tiled=True).reshape(ep_count, 128)
    pair = jnp.concatenate([ids_t.astype(jnp.float32), route_weights.T], axis=0)
    pairs = jnp.concatenate(
        [pair] + [lax.ppermute(pair, "zh", shift(far, -o)) for o in range(1, far)], axis=1
    )
    chosen, pairs = lax.optimization_barrier((chosen.astype(jnp.bfloat16), pairs))

    row = jnp.arange(ep_count * held, dtype=jnp.int32)[:, None]
    r_side = row // (ep_count * exp_dev)
    r_near = row % (ep_count * exp_dev) // (far * exp_dev)
    r_far = row % (far * exp_dev) // exp_dev
    r_exp = row % exp_dev
    zh = lax.axis_index("zh")
    home = (r_near // low * far + (zh + r_far) % far) * low + r_near % low
    homes = jnp.arange(ep_count, dtype=jnp.int32)[None, :]
    before = mul((homes < home).astype(jnp.bfloat16), chosen)
    here = mul((homes == home).astype(jnp.bfloat16), chosen)
    mine = lanes[None, :] == r_side * exp_dev + r_exp
    rank = jnp.sum(jnp.where(mine, before, 0.0), axis=1, keepdims=True)
    hit = jnp.sum(jnp.where(mine, here, 0.0), axis=1, keepdims=True)
    code = jnp.where(hit > 0, rank.astype(jnp.int32) + capacity * r_exp, -1)

    col = jnp.arange(ep_count * held, dtype=jnp.int32)
    c_near = col // (held * far)
    c_side = col % (held * far) // (exp_dev * far)
    c_far = col % (exp_dev * far) // exp_dev
    c_chip = (c_near // low * far + zh) * low + c_near % low
    c_id = (c_side + group) % 2 * per_group + c_chip * exp_dev + col % exp_dev
    ids = jnp.stack([c_id, c_far]).astype(jnp.float32)
    code, ids = lax.optimization_barrier((code, ids))

    outgoing = pick(group.astype(jnp.int32).reshape(1), code, expert_rows, taken, near)
    outgoing, pairs, ids = lax.optimization_barrier((outgoing, pairs, ids))
    rows = lax.all_to_all(outgoing, NEAR, 0, 0, tiled=True)
    rows = rows.reshape(ep_count * held, half)
    partial = combine(pairs, ids, rows).reshape(far, tok_dev, half)
    partial, route_ids, route_weights = lax.optimization_barrier((partial, route_ids, route_weights))
    cut = half // 2
    up, down = shift(far, 1), shift(far, -1)
    far_up = lax.ppermute(partial[2, :, :cut], "zh", up)
    far_down = lax.ppermute(partial[2, :, cut:], "zh", down)
    next_right = lax.ppermute(partial[1, :, cut:], "zh", up)
    prev_left = lax.ppermute(partial[3, :, :cut], "zh", down)
    next_left = lax.ppermute(partial[1, :, :cut] + far_up, "zh", up)
    prev_right = lax.ppermute(partial[3, :, cut:] + far_down, "zh", down)
    total = partial[0] + jnp.concatenate([next_left + prev_left, next_right + prev_right], axis=1)

    ident = jnp.sum(jnp.where(route_ids < experts, 0.0, route_weights), axis=1, keepdims=True)
    return total + ident * lax.dynamic_slice_in_dim(tokens, group * half, half, 1)


def solution(mesh):
    torus = Mesh(mesh.devices.reshape(mesh.shape["grp"], 4, 4, 4, 2), ("grp",) + EP)
    in_specs = (P(EP, None), P(EP, None), P(EP, None), P(("grp",) + EP, None, None))
    return jax.shard_map(
        shards, mesh=torus, in_specs=in_specs, out_specs=P(EP, "grp"), check_vma=False
    )
```

```python
import jax
import jax.numpy as jnp
from jax import lax
from jax.sharding import Mesh
from jax.sharding import PartitionSpec as P
from jax.experimental import pallas as pl
from jax.experimental.pallas import tpu as pltpu

EP = ("x", "y", "zh", "zl")
NEAR = ("x", "y", "zl")
BLOCK = 512
PICK_VMEM = 24 * 1024 * 1024
MIX_VMEM = 24 * 1024 * 1024


def halves(x):
    high = x.astype(jnp.bfloat16)
    rest = x - high.astype(jnp.float32)
    middle = rest.astype(jnp.bfloat16)
    return high, middle, rest - middle.astype(jnp.float32)


def mul(a, b):
    return jnp.dot(a, b, preferred_element_type=jnp.float32)


def pick_kernel(group_ref, chosen_ref, home_ref, lane_ref, own_ref, taken_ref, out_ref, held, arrived):
    sides, steps, exp_dev, capacity, block = held.shape
    start = pl.multiple_of(group_ref[0] * steps * block, block)
    copies = {}
    for i in range(steps):
        for side, ref in enumerate((own_ref, taken_ref)):
            copies[i, side] = pltpu.make_async_copy(
                ref.at[:, :, pl.ds(start + i * block, block)], held.at[side, i], arrived.at[side, i]
            )
            copies[i, side].start()

    chosen = chosen_ref[...].astype(jnp.bfloat16)
    count = home_ref.shape[0]
    homes = lax.broadcasted_iota(jnp.int32, (count, chosen.shape[0]), 1)
    before = mul((homes < home_ref[...]).astype(jnp.float32).astype(jnp.bfloat16), chosen)
    here = mul((homes == home_ref[...]).astype(jnp.float32).astype(jnp.bfloat16), chosen)
    lanes = lax.broadcasted_iota(jnp.int32, before.shape, 1)
    expert = lax.rem(lane_ref[...], exp_dev)
    code = jnp.where(here > 0, before.astype(jnp.int32) + capacity * expert, -1)
    code = jnp.sum(jnp.where(lanes == lane_ref[...], code, 0), axis=1, keepdims=True)
    slot = lax.broadcasted_iota(jnp.int32, (count, exp_dev * capacity), 1)
    select = (code == slot).astype(jnp.float32).astype(jnp.bfloat16)

    targets, rows, _ = out_ref.shape
    each = count // sides
    for i in range(steps):
        for side in range(sides):
            copies[i, side].wait()
            table = held[side, i].reshape(exp_dev * capacity, block)
            high, middle, rest = halves(table)
            mine = select[side * each : (side + 1) * each, :]
            value = mul(mine, high) + mul(mine, middle) + mul(mine, rest.astype(jnp.bfloat16))
            out_ref[:, side * rows // 2 : (side + 1) * rows // 2, i * block : (i + 1) * block] = value.reshape(
                targets, rows // 2, block
            )


def pick(group, chosen, home, lane, own, taken, targets):
    exp_dev, capacity, width = own.shape
    half = width // 2
    steps = half // BLOCK
    count = home.shape[0]
    slots = exp_dev * capacity
    vmem = pl.BlockSpec(memory_space=pltpu.VMEM)
    hbm = pl.BlockSpec(memory_space=pl.ANY)
    return pl.pallas_call(
        pick_kernel,
        out_shape=jax.ShapeDtypeStruct((targets, count // targets, half), jnp.float32),
        in_specs=[pl.BlockSpec(memory_space=pltpu.SMEM), vmem, vmem, vmem, hbm, hbm],
        out_specs=vmem,
        scratch_shapes=[
            pltpu.VMEM((2, steps, exp_dev, capacity, BLOCK), jnp.float32),
            pltpu.SemaphoreType.DMA((2, steps)),
        ],
        compiler_params=pltpu.CompilerParams(vmem_limit_bytes=PICK_VMEM),
        cost_estimate=pl.CostEstimate(
            flops=6 * count * slots * half, bytes_accessed=4 * (2 * slots + count) * half, transcendentals=0
        ),
        name="pick",
    )(group, chosen, home, lane, own, taken)


def combine_kernel(*refs):
    pair_refs, (ids_ref, rows_ref, out_ref) = refs[:-3], refs[-3:]
    pairs = jnp.concatenate([ref[...].T for ref in pair_refs], axis=0)
    count = pairs.shape[0]
    top = pairs.shape[1] // 2
    ids = ids_ref[0:1, :]
    total = jnp.zeros((count, rows_ref.shape[0]), jnp.float32)
    for k in range(top):
        total += jnp.where(pairs[:, k : k + 1] == ids, pairs[:, top + k : top + k + 1], 0.0)
    line = lax.broadcasted_iota(jnp.int32, total.shape, 0) * len(pair_refs) // count
    total = jnp.where(line.astype(jnp.float32) == ids_ref[1:2, :], total, 0.0)
    m_high, m_middle, _ = halves(total)
    both = jnp.concatenate([m_high, m_middle], axis=0)
    for i in range(rows_ref.shape[1] // BLOCK):
        here = slice(i * BLOCK, (i + 1) * BLOCK)
        high, middle, _ = halves(rows_ref[:, here])
        value = mul(both, high)
        out_ref[:, here] = value[:count] + (value[count:] + mul(m_high, middle))


def combine(pairs, ids, rows):
    count = len(pairs) * pairs[0].shape[1]
    depth, half = rows.shape
    return pl.pallas_call(
        combine_kernel,
        out_shape=jax.ShapeDtypeStruct((count, half), jnp.float32),
        in_specs=[pl.BlockSpec(memory_space=pltpu.VMEM)] * (len(pairs) + 2),
        out_specs=pl.BlockSpec(memory_space=pltpu.VMEM),
        compiler_params=pltpu.CompilerParams(vmem_limit_bytes=MIX_VMEM),
        cost_estimate=pl.CostEstimate(
            flops=6 * count * depth * half, bytes_accessed=4 * (count + depth) * half, transcendentals=0
        ),
        name="combine",
    )(*pairs, ids, rows)


def shift(count, by):
    return [(i, (i + by) % count) for i in range(count)]


def shards(tokens, route_ids, route_weights, expert_rows):
    group = lax.axis_index("grp")
    ep_count = lax.axis_size(EP)
    far = lax.axis_size("zh")
    low = lax.axis_size("zl")
    near = ep_count // far
    tok_dev, top = route_ids.shape
    exp_dev, capacity, width = expert_rows.shape
    half = width // 2
    held = 2 * exp_dev
    per_group = exp_dev * ep_count
    experts = 2 * per_group

    taken = lax.ppermute(expert_rows, "grp", [(0, 1), (1, 0)])

    ids_t = route_ids.T
    chip = jnp.where(ids_t < experts, ids_t % per_group // exp_dev, -1)
    place = (ids_t // per_group != group) * exp_dev + ids_t % exp_dev
    lanes = jnp.arange(128, dtype=jnp.int32)
    chip_hot = (chip[:, :, None] == jnp.arange(ep_count, dtype=jnp.int32)).astype(jnp.bfloat16)
    place_hot = (place[:, :, None] == lanes).astype(jnp.bfloat16)
    flags = lax.dot_general(
        chip_hot.reshape(top * tok_dev, ep_count), place_hot.reshape(top * tok_dev, 128),
        (((0,), (0,)), ((), ())), preferred_element_type=jnp.float32,
    )
    chosen = lax.all_to_all(flags[:, None, :], EP, 0, 0, tiled=True).reshape(ep_count, 128)

    row = jnp.arange(ep_count * held, dtype=jnp.int32)[:, None]
    r_side = row // (ep_count * exp_dev)
    r_near = row % (ep_count * exp_dev) // (far * exp_dev)
    r_far = row % (far * exp_dev) // exp_dev
    r_exp = row % exp_dev
    zh = lax.axis_index("zh")
    home = (r_near // low * far + (zh + r_far) % far) * low + r_near % low
    lane = r_side * exp_dev + r_exp

    col = jnp.arange(ep_count * held, dtype=jnp.int32)
    c_near = col // (held * far)
    c_side = col % (held * far) // (exp_dev * far)
    c_far = col % (exp_dev * far) // exp_dev
    c_chip = (c_near // low * far + zh) * low + c_near % low
    c_id = (c_side + group) % 2 * per_group + c_chip * exp_dev + col % exp_dev
    ids = jnp.stack([c_id, c_far]).astype(jnp.float32)

    pair = jnp.concatenate([ids_t.astype(jnp.float32), route_weights.T], axis=0)
    chosen, pair, ids, home, lane = lax.optimization_barrier((chosen, pair, ids, home, lane))
    pairs = [pair] + [lax.ppermute(pair, "zh", shift(far, -o)) for o in range(1, far)]
    outgoing = pick(group.astype(jnp.int32).reshape(1), chosen, home, lane, pltpu.with_memory_space_constraint(expert_rows, pltpu.HBM), taken, near)
    outgoing, pairs, ids = lax.optimization_barrier((outgoing, pairs, ids))
    rows = lax.all_to_all(outgoing, NEAR, 0, 0, tiled=True)
    rows = rows.reshape(ep_count * held, half)
    partial = combine(pairs, ids, rows).reshape(far, tok_dev, half)
    partial, route_ids, route_weights = lax.optimization_barrier((partial, route_ids, route_weights))
    cut = half // 2
    up, down = shift(far, 1), shift(far, -1)
    far_up = lax.ppermute(partial[2, :, :cut], "zh", up)
    far_down = lax.ppermute(partial[2, :, cut:], "zh", down)
    next_right = lax.ppermute(partial[1, :, cut:], "zh", up)
    prev_left = lax.ppermute(partial[3, :, :cut], "zh", down)
    next_left = lax.ppermute(partial[1, :, :cut] + far_up, "zh", up)
    prev_right = lax.ppermute(partial[3, :, cut:] + far_down, "zh", down)
    total = partial[0] + jnp.concatenate([next_left + prev_left, next_right + prev_right], axis=1)

    ident = jnp.sum(jnp.where(route_ids < experts, 0.0, route_weights), axis=1, keepdims=True)
    return total + ident * lax.dynamic_slice_in_dim(tokens, group * half, half, 1)


def solution(mesh):
    torus = Mesh(mesh.devices.reshape(mesh.shape["grp"], 4, 4, 4, 2), ("grp",) + EP)
    in_specs = (P(EP, None), P(EP, None), P(EP, None), P(("grp",) + EP, None, None))
    return jax.shard_map(
        shards, mesh=torus, in_specs=in_specs, out_specs=P(EP, "grp"), check_vma=False
    )
```

```python
import functools

import jax
import jax.numpy as jnp
from jax import lax
from jax.sharding import Mesh
from jax.sharding import PartitionSpec as P
from jax.experimental import pallas as pl
from jax.experimental.pallas import tpu as pltpu

EP = ("x", "y", "zh", "zl")
NEAR = ("x", "y", "zl")
BLOCK = 512
PICK_VMEM = 24 * 1024 * 1024
MIX_VMEM = 24 * 1024 * 1024


def halves(x):
    high = x.astype(jnp.bfloat16)
    rest = x - high.astype(jnp.float32)
    middle = rest.astype(jnp.bfloat16)
    return high, middle, rest - middle.astype(jnp.float32)


def mul(a, b):
    return jnp.dot(a, b, preferred_element_type=jnp.float32)


def ask_kernel(group_ref, ids_ref, weights_ref, out_ref, both, *, exp_dev, per_group):
    top, count = ids_ref.shape
    chips = out_ref.shape[0]
    gap = 2 * exp_dev
    second = both.shape[0] // 2
    ids = ids_ref[...]
    chip = jnp.where(ids < 2 * per_group, lax.div(lax.rem(ids, per_group), exp_dev), -1)
    both[...] = jnp.zeros_like(both)
    both[0:top, :] = ids.astype(jnp.float32)
    both[second : second + top, :] = weights_ref[...]
    columns = both[...].T
    chip_lines = lax.broadcasted_iota(jnp.int32, (chips, count), 0)
    lanes = lax.broadcasted_iota(jnp.int32, (count, 128), 1)
    token = (lax.broadcasted_iota(jnp.int32, (count, 128), 0) + 1).astype(jnp.float32)
    total = jnp.zeros((chips, 128), jnp.float32)
    for k in range(top):
        names = columns[:, k : k + 1].astype(jnp.int32)
        place = jnp.where(lax.div(names, per_group) == group_ref[0], 0, exp_dev) + lax.rem(names, exp_dev)
        high, middle, low = halves(columns[:, second + k : second + k + 1])
        value = jnp.where(lanes == place, token, 0.0)
        value = jnp.where(lanes == place + gap, high.astype(jnp.float32), value)
        value = jnp.where(lanes == place + 2 * gap, middle.astype(jnp.float32), value)
        value = jnp.where(lanes == place + 3 * gap, low, value)
        where = (chip_lines == chip[k : k + 1, :]).astype(jnp.float32).astype(jnp.bfloat16)
        total += mul(where, value.astype(jnp.bfloat16))
    weight = total + pltpu.roll(total, 128 - gap, 1) + pltpu.roll(total, 128 - 2 * gap, 1)
    lanes = lax.broadcasted_iota(jnp.int32, total.shape, 1)
    out_ref[...] = jnp.where(lanes < gap, total, jnp.where(lanes < 2 * gap, weight, 0.0))


def ask(group, ids, weights, chips, exp_dev, per_group):
    top, count = ids.shape
    vmem = pl.BlockSpec(memory_space=pltpu.VMEM)
    return pl.pallas_call(
        functools.partial(ask_kernel, exp_dev=exp_dev, per_group=per_group),
        out_shape=jax.ShapeDtypeStruct((chips, 128), jnp.float32),
        in_specs=[pl.BlockSpec(memory_space=pltpu.SMEM), vmem, vmem],
        out_specs=vmem,
        scratch_shapes=[pltpu.VMEM((2 * (-(-top // 8) * 8), count), jnp.float32)],
        compiler_params=pltpu.CompilerParams(vmem_limit_bytes=MIX_VMEM),
        name="ask",
    )(group, ids, weights)


def pick_kernel(group_ref, chosen_ref, home_ref, lane_ref, own_ref, taken_ref, out_ref, held, arrived):
    sides, steps, exp_dev, capacity, block = held.shape
    start = pl.multiple_of(group_ref[0] * steps * block, block)
    copies = {}
    for i in range(steps):
        for side, ref in enumerate((own_ref, taken_ref)):
            copies[i, side] = pltpu.make_async_copy(
                ref.at[:, :, pl.ds(start + i * block, block)], held.at[side, i], arrived.at[side, i]
            )
            copies[i, side].start()

    chosen = chosen_ref[...]
    count = home_ref.shape[0]
    gap = sides * exp_dev
    homes = lax.broadcasted_iota(jnp.int32, (count, chosen.shape[0]), 1)
    earlier = (homes < home_ref[...]).astype(jnp.float32).astype(jnp.bfloat16)
    before = mul(earlier, (chosen > 0).astype(jnp.float32).astype(jnp.bfloat16))
    high, middle, low = halves(chosen)
    this = (homes == home_ref[...]).astype(jnp.float32).astype(jnp.bfloat16)
    here = mul(this, high) + mul(this, middle) + mul(this, low.astype(jnp.bfloat16))
    lanes = lax.broadcasted_iota(jnp.int32, here.shape, 1)
    mine = lanes == lane_ref[...]
    token = jnp.sum(jnp.where(mine, here, 0.0), axis=1, keepdims=True)
    weight = jnp.sum(jnp.where(lanes == lane_ref[...] + gap, here, 0.0), axis=1, keepdims=True)
    rank = jnp.sum(jnp.where(mine, before, 0.0), axis=1, keepdims=True)
    code = jnp.where(token > 0, rank.astype(jnp.int32) + capacity * lax.rem(lane_ref[...], exp_dev), -1)
    slot = lax.broadcasted_iota(jnp.int32, (count, exp_dev * capacity), 1)
    select = (code == slot).astype(jnp.float32).astype(jnp.bfloat16)

    targets, lines, group = out_ref.shape
    each = count // sides
    rows = each // targets
    lanes = lanes[:each]
    note = jnp.where(lanes == 0, token[:each], jnp.where(lanes == 1, weight[:each], 0.0))
    note = jnp.where(lanes == 2, token[each:], jnp.where(lanes == 3, weight[each:], note))
    out_ref[:, lines - rows :, :] = note.reshape(targets, rows, group)
    per = block // group
    for i in range(steps):
        for side in range(sides):
            copies[i, side].wait()
            high, middle, _ = halves(held[side, i].reshape(exp_dev * capacity, block))
            wanted = select[side * each : (side + 1) * each, :]
            value = mul(wanted, high) + mul(wanted, middle)
            for j in range(per):
                line = ((i * per + j) * sides + side) * rows
                out_ref[:, line : line + rows, :] = value[:, j * group : (j + 1) * group].reshape(targets, rows, group)


def pick(group, chosen, home, lane, own, taken, targets):
    exp_dev, capacity, width = own.shape
    half = width // 2
    steps = half // BLOCK
    count = home.shape[0]
    slots = exp_dev * capacity
    lines = count // targets * half // 128 + count // targets // 2
    vmem = pl.BlockSpec(memory_space=pltpu.VMEM)
    hbm = pl.BlockSpec(memory_space=pl.ANY)
    return pl.pallas_call(
        pick_kernel,
        out_shape=jax.ShapeDtypeStruct((targets, lines, 128), jnp.float32),
        in_specs=[pl.BlockSpec(memory_space=pltpu.SMEM), vmem, vmem, vmem, hbm, hbm],
        out_specs=vmem,
        scratch_shapes=[
            pltpu.VMEM((2, steps, exp_dev, capacity, BLOCK), jnp.float32),
            pltpu.SemaphoreType.DMA((2, steps)),
        ],
        compiler_params=pltpu.CompilerParams(vmem_limit_bytes=PICK_VMEM),
        cost_estimate=pl.CostEstimate(
            flops=4 * count * slots * half, bytes_accessed=4 * (2 * slots + count) * half, transcendentals=0
        ),
        name="pick",
    )(group, chosen, home, lane, own, taken)


def combine_kernel(rows_ref, out_ref, *, far, exp_dev):
    sources, lines, group = rows_ref.shape
    rows = far * exp_dev
    count, half = out_ref.shape
    note = rows_ref[:, lines - rows :, :].reshape(sources * rows, group)
    line = lax.broadcasted_iota(jnp.int32, (sources * rows, count), 0)
    out_line = lax.broadcasted_iota(jnp.int32, (sources * rows, count), 1)
    right = lax.div(lax.rem(line, rows), exp_dev) == lax.div(out_line, count // far)
    token = jnp.where(right, lax.rem(out_line, count // far) + 1, -1).astype(jnp.float32)
    sides = []
    for side in range(2):
        named = note[:, 2 * side : 2 * side + 1] == token
        mix = jnp.where(named, note[:, 2 * side + 1 : 2 * side + 2], 0.0)
        sides.append(mix.reshape(sources, rows, count))
    mix = jnp.concatenate(sides, axis=1).reshape(2 * sources * rows, count).T
    m_high, m_middle, _ = halves(mix)
    both = jnp.concatenate([m_high, m_middle], axis=0)
    per = BLOCK // group
    for i in range(half // BLOCK):
        parts = [rows_ref[:, 2 * rows * (i * per + j) : 2 * rows * (i * per + j + 1), :] for j in range(per)]
        block = jnp.concatenate([part.reshape(2 * sources * rows, group) for part in parts], axis=1)
        high, middle, _ = halves(block)
        value = mul(both, high)
        out_ref[:, i * BLOCK : (i + 1) * BLOCK] = value[:count] + (value[count:] + mul(m_high, middle))


def combine(rows, far, exp_dev, tok_dev, half):
    count = far * tok_dev
    depth = 2 * rows.shape[0] * far * exp_dev
    return pl.pallas_call(
        functools.partial(combine_kernel, far=far, exp_dev=exp_dev),
        out_shape=jax.ShapeDtypeStruct((count, half), jnp.float32),
        in_specs=[pl.BlockSpec(memory_space=pltpu.VMEM)],
        out_specs=pl.BlockSpec(memory_space=pltpu.VMEM),
        compiler_params=pltpu.CompilerParams(vmem_limit_bytes=MIX_VMEM),
        cost_estimate=pl.CostEstimate(
            flops=6 * count * depth * half, bytes_accessed=4 * (count + depth) * half, transcendentals=0
        ),
        name="combine",
    )(rows)


def shift(count, by):
    return [(i, (i + by) % count) for i in range(count)]


def shards(tokens, route_ids, route_weights, expert_rows):
    group = lax.axis_index("grp")
    ep_count = lax.axis_size(EP)
    far = lax.axis_size("zh")
    low = lax.axis_size("zl")
    near = ep_count // far
    tok_dev, top = route_ids.shape
    exp_dev, capacity, width = expert_rows.shape
    half = width // 2
    held = 2 * exp_dev
    per_group = exp_dev * ep_count
    experts = 2 * per_group

    taken = lax.ppermute(expert_rows, "grp", [(0, 1), (1, 0)])

    group_word = group.astype(jnp.int32).reshape(1)
    asked = ask(group_word, route_ids.T, route_weights.T, ep_count, exp_dev, per_group)
    chosen = lax.all_to_all(asked[:, None, :], EP, 0, 0, tiled=True).reshape(ep_count, 128)

    row = jnp.arange(ep_count * held, dtype=jnp.int32)[:, None]
    r_side = row // (ep_count * exp_dev)
    r_near = row % (ep_count * exp_dev) // (far * exp_dev)
    r_far = row % (far * exp_dev) // exp_dev
    r_exp = row % exp_dev
    zh = lax.axis_index("zh")
    home = (r_near // low * far + (zh + r_far) % far) * low + r_near % low
    lane = r_side * exp_dev + r_exp

    chosen, home, lane, taken = lax.optimization_barrier((chosen, home, lane, taken))
    own = pltpu.with_memory_space_constraint(expert_rows, pltpu.HBM)
    outgoing = pick(group_word, chosen, home, lane, own, taken, near)

    rows = lax.all_to_all(outgoing, NEAR, 0, 0, tiled=True)
    partial = combine(rows, far, exp_dev, tok_dev, half).reshape(far, tok_dev, half)
    partial, route_ids, route_weights = lax.optimization_barrier((partial, route_ids, route_weights))
    cut = half // 2
    up, down = shift(far, 1), shift(far, -1)
    far_up = lax.ppermute(partial[2, :, :cut], "zh", up)
    far_down = lax.ppermute(partial[2, :, cut:], "zh", down)
    next_right = lax.ppermute(partial[1, :, cut:], "zh", up)
    prev_left = lax.ppermute(partial[3, :, :cut], "zh", down)
    next_left = lax.ppermute(partial[1, :, :cut] + far_up, "zh", up)
    prev_right = lax.ppermute(partial[3, :, cut:] + far_down, "zh", down)
    total = partial[0] + jnp.concatenate([next_left + prev_left, next_right + prev_right], axis=1)

    ident = jnp.sum(jnp.where(route_ids < experts, 0.0, route_weights), axis=1, keepdims=True)
    return total + ident * lax.dynamic_slice_in_dim(tokens, group * half, half, 1)


def solution(mesh):
    torus = Mesh(mesh.devices.reshape(mesh.shape["grp"], 4, 4, 4, 2), ("grp",) + EP)
    in_specs = (P(EP, None), P(EP, None), P(EP, None), P(("grp",) + EP, None, None))
    return jax.shard_map(
        shards, mesh=torus, in_specs=in_specs, out_specs=P(EP, "grp"), check_vma=False
    )
```

```python
import functools

import jax
import jax.numpy as jnp
from jax import lax
from jax.sharding import Mesh
from jax.sharding import PartitionSpec as P
from jax.experimental import pallas as pl
from jax.experimental.pallas import tpu as pltpu

EP = ("x", "y", "zh", "zl")
NEAR = ("x", "y", "zl")
BLOCK = 512
PICK_VMEM = 24 * 1024 * 1024
MIX_VMEM = 24 * 1024 * 1024


def halves(x):
    high = x.astype(jnp.bfloat16)
    rest = x - high.astype(jnp.float32)
    middle = rest.astype(jnp.bfloat16)
    return high, middle, rest - middle.astype(jnp.float32)


def in_hbm(x):
    return pltpu.with_memory_space_constraint(x, pltpu.HBM)


def mul(a, b):
    return jnp.dot(a, b, preferred_element_type=jnp.float32)


def ask_kernel(
    group_ref, ids_hbm, weights_hbm, out_ref, ident_ref, ids_ref, weights_ref, both, arrived, *, exp_dev, per_group
):
    copies = [
        pltpu.make_async_copy(ids_hbm, ids_ref, arrived.at[0]),
        pltpu.make_async_copy(weights_hbm, weights_ref, arrived.at[1]),
    ]
    for copy in copies:
        copy.start()
    for copy in copies:
        copy.wait()
    top, count = ids_ref.shape
    chips = out_ref.shape[0]
    gap = 2 * exp_dev
    second = both.shape[0] // 2
    ids = ids_ref[...]
    chip = jnp.where(ids < 2 * per_group, lax.div(lax.rem(ids, per_group), exp_dev), -1)
    both[...] = jnp.zeros_like(both)
    both[0:top, :] = ids.astype(jnp.float32)
    both[second : second + top, :] = weights_ref[...]
    columns = both[...].T
    chip_lines = lax.broadcasted_iota(jnp.int32, (chips, count), 0)
    lanes = lax.broadcasted_iota(jnp.int32, (count, 128), 1)
    token = (lax.broadcasted_iota(jnp.int32, (count, 128), 0) + 1).astype(jnp.float32)
    total = jnp.zeros((chips, 128), jnp.float32)
    ident = jnp.zeros((count, 1), jnp.float32)
    for k in range(top):
        names = columns[:, k : k + 1].astype(jnp.int32)
        ident += jnp.where(names < 2 * per_group, 0.0, columns[:, second + k : second + k + 1])
        place = jnp.where(lax.div(names, per_group) == group_ref[0], 0, exp_dev) + lax.rem(names, exp_dev)
        high, middle, low = halves(columns[:, second + k : second + k + 1])
        value = jnp.where(lanes == place, token, 0.0)
        value = jnp.where(lanes == place + gap, high.astype(jnp.float32), value)
        value = jnp.where(lanes == place + 2 * gap, middle.astype(jnp.float32), value)
        value = jnp.where(lanes == place + 3 * gap, low, value)
        where = (chip_lines == chip[k : k + 1, :]).astype(jnp.float32).astype(jnp.bfloat16)
        total += mul(where, value.astype(jnp.bfloat16))
    ident_ref[...] = jnp.broadcast_to(ident, ident_ref.shape)
    weight = total + pltpu.roll(total, 128 - gap, 1) + pltpu.roll(total, 128 - 2 * gap, 1)
    lanes = lax.broadcasted_iota(jnp.int32, total.shape, 1)
    out_ref[...] = jnp.where(lanes < gap, total, jnp.where(lanes < 2 * gap, weight, 0.0))


def ask(group, ids, weights, chips, exp_dev, per_group):
    top, count = ids.shape
    vmem = pl.BlockSpec(memory_space=pltpu.VMEM)
    hbm = pl.BlockSpec(memory_space=pl.ANY)
    return pl.pallas_call(
        functools.partial(ask_kernel, exp_dev=exp_dev, per_group=per_group),
        out_shape=(
            jax.ShapeDtypeStruct((chips, 128), jnp.float32),
            jax.ShapeDtypeStruct((count, 128), jnp.float32),
        ),
        in_specs=[pl.BlockSpec(memory_space=pltpu.SMEM), hbm, hbm],
        out_specs=(vmem, vmem),
        scratch_shapes=[
            pltpu.VMEM((top, count), jnp.int32),
            pltpu.VMEM((top, count), jnp.float32),
            pltpu.VMEM((2 * (-(-top // 8) * 8), count), jnp.float32),
            pltpu.SemaphoreType.DMA((2,)),
        ],
        compiler_params=pltpu.CompilerParams(vmem_limit_bytes=MIX_VMEM),
        name="ask",
    )(group, in_hbm(ids), in_hbm(weights))


def pick_kernel(group_ref, chosen_ref, home_ref, lane_ref, own_ref, taken_ref, out_ref, held, arrived):
    sides, steps, exp_dev, capacity, block = held.shape
    start = pl.multiple_of(group_ref[0] * steps * block, block)
    copies = {}
    for i in range(steps):
        for side, ref in enumerate((own_ref, taken_ref)):
            copies[i, side] = pltpu.make_async_copy(
                ref.at[:, :, pl.ds(start + i * block, block)], held.at[side, i], arrived.at[side, i]
            )
            copies[i, side].start()

    chosen = chosen_ref[...]
    count = home_ref.shape[0]
    gap = sides * exp_dev
    homes = lax.broadcasted_iota(jnp.int32, (count, chosen.shape[0]), 1)
    earlier = (homes < home_ref[...]).astype(jnp.float32).astype(jnp.bfloat16)
    before = mul(earlier, (chosen > 0).astype(jnp.float32).astype(jnp.bfloat16))
    high, middle, low = halves(chosen)
    home_lanes = lax.broadcasted_iota(jnp.int32, chosen.shape, 1)
    packed = jnp.where(home_lanes < 4 * gap, pltpu.roll(middle.astype(jnp.float32), 2 * gap, 1), pltpu.roll(low, 4 * gap, 1))
    packed = jnp.where(home_lanes < 2 * gap, high.astype(jnp.float32), packed)
    this = (homes == home_ref[...]).astype(jnp.float32).astype(jnp.bfloat16)
    here = mul(this, packed.astype(jnp.bfloat16))
    lanes = lax.broadcasted_iota(jnp.int32, here.shape, 1)
    mine = lanes == lane_ref[...]
    token = jnp.sum(jnp.where(mine, here, 0.0), axis=1, keepdims=True)
    parts = (lax.rem(lanes, 2 * gap) == lane_ref[...] + gap) & (lanes < 6 * gap)
    weight = jnp.sum(jnp.where(parts, here, 0.0), axis=1, keepdims=True)
    rank = jnp.sum(jnp.where(mine, before, 0.0), axis=1, keepdims=True)
    code = jnp.where(token > 0, rank.astype(jnp.int32) + capacity * lax.rem(lane_ref[...], exp_dev), -1)
    slot = lax.broadcasted_iota(jnp.int32, (count, exp_dev * capacity), 1)
    select = (code == slot).astype(jnp.float32).astype(jnp.bfloat16)

    targets, lines, group = out_ref.shape
    each = count // sides
    rows = each // targets
    lanes = lanes[:each]
    note = jnp.where(lanes == 0, token[:each], jnp.where(lanes == 1, weight[:each], 0.0))
    note = jnp.where(lanes == 2, token[each:], jnp.where(lanes == 3, weight[each:], note))
    out_ref[:, lines - rows :, :] = note.reshape(targets, rows, group)
    per = block // group
    for i in range(steps):
        for side in range(sides):
            copies[i, side].wait()
            high, middle, _ = halves(held[side, i].reshape(exp_dev * capacity, block))
            wanted = select[side * each : (side + 1) * each, :]
            value = mul(wanted, high) + mul(wanted, middle)
            for j in range(per):
                line = ((i * per + j) * sides + side) * rows
                out_ref[:, line : line + rows, :] = value[:, j * group : (j + 1) * group].reshape(targets, rows, group)


def pick(group, chosen, home, lane, own, taken, targets):
    exp_dev, capacity, width = own.shape
    half = width // 2
    steps = half // BLOCK
    count = home.shape[0]
    slots = exp_dev * capacity
    lines = count // targets * half // 128 + count // targets // 2
    vmem = pl.BlockSpec(memory_space=pltpu.VMEM)
    hbm = pl.BlockSpec(memory_space=pl.ANY)
    return pl.pallas_call(
        pick_kernel,
        out_shape=jax.ShapeDtypeStruct((targets, lines, 128), jnp.float32),
        in_specs=[pl.BlockSpec(memory_space=pltpu.SMEM), vmem, vmem, vmem, hbm, hbm],
        out_specs=vmem,
        scratch_shapes=[
            pltpu.VMEM((2, steps, exp_dev, capacity, BLOCK), jnp.float32),
            pltpu.SemaphoreType.DMA((2, steps)),
        ],
        compiler_params=pltpu.CompilerParams(vmem_limit_bytes=PICK_VMEM),
        cost_estimate=pl.CostEstimate(
            flops=4 * count * slots * half, bytes_accessed=4 * (2 * slots + count) * half, transcendentals=0
        ),
        name="pick",
    )(group, chosen, home, lane, own, taken)


def combine_kernel(
    group_ref, rows_ref, ident_ref, tokens_ref, base_ref, up_ref, down_ref, left_ref, right_ref, own, arrived, *, exp_dev
):
    tok_dev, half = base_ref.shape
    copy = pltpu.make_async_copy(
        tokens_ref.at[:, pl.ds(pl.multiple_of(group_ref[0] * half, half), half)], own, arrived
    )
    copy.start()
    sources, lines, group = rows_ref.shape
    far = 4
    rows = far * exp_dev
    count = far * tok_dev
    note = rows_ref[:, lines - rows :, :].reshape(sources * rows, group)
    line = lax.broadcasted_iota(jnp.int32, (sources * rows, count), 0)
    out_line = lax.broadcasted_iota(jnp.int32, (sources * rows, count), 1)
    fits = lax.div(lax.rem(line, rows), exp_dev) == lax.div(out_line, tok_dev)
    token = jnp.where(fits, lax.rem(out_line, tok_dev) + 1, -1).astype(jnp.float32)
    sides = []
    for side in range(2):
        named = note[:, 2 * side : 2 * side + 1] == token
        mix = jnp.where(named, note[:, 2 * side + 1 : 2 * side + 2], 0.0)
        sides.append(mix.reshape(sources, rows, count))
    mix = jnp.concatenate(sides, axis=1).reshape(2 * sources * rows, count).T
    m_high, m_middle, _ = halves(mix)
    both = jnp.concatenate([m_high, m_middle], axis=0)
    per = BLOCK // group
    steps = half // BLOCK
    copy.wait()
    ident = ident_ref[:, 0:1]
    for i in range(steps):
        parts = [rows_ref[:, 2 * rows * (i * per + j) : 2 * rows * (i * per + j + 1), :] for j in range(per)]
        block = jnp.concatenate([part.reshape(2 * sources * rows, group) for part in parts], axis=1)
        high, middle, _ = halves(block)
        value = mul(both, high)
        value = value[:count] + (value[count:] + mul(m_high, middle))
        near, nxt, opposite, prev = (value[o * tok_dev : (o + 1) * tok_dev] for o in range(far))
        here = slice(i * BLOCK, (i + 1) * BLOCK)
        base_ref[:, here] = near + ident * own[:, here]
        side = slice(i % (steps // 2) * BLOCK, (i % (steps // 2) + 1) * BLOCK)
        if i < steps // 2:
            up_ref[:tok_dev, side] = opposite
            down_ref[tok_dev:, side] = prev
            left_ref[:, side] = nxt
        else:
            down_ref[:tok_dev, side] = opposite
            up_ref[tok_dev:, side] = nxt
            right_ref[:, side] = prev


def combine(group, rows, ident, tokens, exp_dev):
    tok_dev, width = tokens.shape
    half = width // 2
    count, depth = 4 * tok_dev, 8 * rows.shape[0] * exp_dev
    vmem = pl.BlockSpec(memory_space=pltpu.VMEM)
    return pl.pallas_call(
        functools.partial(combine_kernel, exp_dev=exp_dev),
        out_shape=[
            jax.ShapeDtypeStruct(shape, jnp.float32)
            for shape in ((tok_dev, half), *[(2 * tok_dev, half // 2)] * 2, *[(tok_dev, half // 2)] * 2)
        ],
        in_specs=[pl.BlockSpec(memory_space=pltpu.SMEM), vmem, vmem, pl.BlockSpec(memory_space=pl.ANY)],
        out_specs=[vmem] * 5,
        scratch_shapes=[pltpu.VMEM((tok_dev, half), jnp.float32), pltpu.SemaphoreType.DMA],
        compiler_params=pltpu.CompilerParams(vmem_limit_bytes=MIX_VMEM),
        cost_estimate=pl.CostEstimate(
            flops=6 * count * depth * half, bytes_accessed=4 * (count + depth) * half, transcendentals=0
        ),
        name="combine",
    )(group, rows, ident, in_hbm(tokens))


def finish_kernel(base_ref, up_ref, down_ref, left_ref, right_ref, out_ref):
    tok_dev, cut = left_ref.shape
    out_ref[:, :cut] = base_ref[:, :cut] + down_ref[tok_dev:, :] + left_ref[...]
    out_ref[:, cut:] = base_ref[:, cut:] + up_ref[tok_dev:, :] + right_ref[...]


def finish(base, *parts):
    vmem = pl.BlockSpec(memory_space=pltpu.VMEM)
    return pl.pallas_call(
        finish_kernel,
        out_shape=jax.ShapeDtypeStruct(base.shape, jnp.float32),
        in_specs=[vmem] * 5,
        out_specs=vmem,
        compiler_params=pltpu.CompilerParams(vmem_limit_bytes=MIX_VMEM),
        name="finish",
    )(base, *parts)


def shift(count, by):
    return [(i, (i + by) % count) for i in range(count)]


def shards(tokens, route_ids, route_weights, expert_rows):
    group = lax.axis_index("grp")
    ep_count = lax.axis_size(EP)
    far = lax.axis_size("zh")
    low = lax.axis_size("zl")
    near = ep_count // far
    tok_dev, top = route_ids.shape
    exp_dev, capacity, width = expert_rows.shape
    half = width // 2
    held = 2 * exp_dev
    per_group = exp_dev * ep_count
    experts = 2 * per_group

    taken = lax.ppermute(expert_rows, "grp", [(0, 1), (1, 0)])

    group_word = group.astype(jnp.int32).reshape(1)
    asked, ident = ask(group_word, route_ids.T, route_weights.T, ep_count, exp_dev, per_group)
    chosen = lax.all_to_all(asked[:, None, :], EP, 0, 0, tiled=True).reshape(ep_count, 128)

    row = jnp.arange(ep_count * held, dtype=jnp.int32)[:, None]
    r_side = row // (ep_count * exp_dev)
    r_near = row % (ep_count * exp_dev) // (far * exp_dev)
    r_far = row % (far * exp_dev) // exp_dev
    r_exp = row % exp_dev
    zh = lax.axis_index("zh")
    home = (r_near // low * far + (zh + r_far) % far) * low + r_near % low
    lane = r_side * exp_dev + r_exp

    chosen, home, lane, taken = lax.optimization_barrier((chosen, home, lane, taken))
    outgoing = pick(group_word, chosen, home, lane, in_hbm(expert_rows), taken, near)

    rows = lax.all_to_all(outgoing, NEAR, 0, 0, tiled=True)
    up, down = shift(far, 1), shift(far, -1)
    base, to_up, to_down, left, right = combine(group_word, rows, ident, tokens, exp_dev)
    from_up, from_down = lax.ppermute(to_up, "zh", up), lax.ppermute(to_down, "zh", down)
    left = lax.ppermute(left + from_up[:tok_dev], "zh", up)
    right = lax.ppermute(right + from_down[:tok_dev], "zh", down)
    return finish(base, from_up, from_down, left, right)


def solution(mesh):
    torus = Mesh(mesh.devices.reshape(mesh.shape["grp"], 4, 4, 4, 2), ("grp",) + EP)
    in_specs = (P(EP, None), P(EP, None), P(EP, None), P(("grp",) + EP, None, None))
    return jax.shard_map(
        shards, mesh=torus, in_specs=in_specs, out_specs=P(EP, "grp"), check_vma=False
    )
```

```python
import functools

import jax
import jax.numpy as jnp
from jax import lax
from jax.sharding import Mesh
from jax.sharding import PartitionSpec as P
from jax.experimental import pallas as pl
from jax.experimental.pallas import tpu as pltpu

EP = ("x", "y", "zh", "zl")
NEAR = ("x", "y", "zl")
BLOCK = 512
PICK_VMEM = 24 * 1024 * 1024
MIX_VMEM = 24 * 1024 * 1024


def halves(x):
    high = x.astype(jnp.bfloat16)
    rest = x - high.astype(jnp.float32)
    middle = rest.astype(jnp.bfloat16)
    return high, middle, rest - middle.astype(jnp.float32)


def in_hbm(x):
    return pltpu.with_memory_space_constraint(x, pltpu.HBM)


def mul(a, b):
    return jnp.dot(a, b, preferred_element_type=jnp.float32)


def ask_kernel(
    group_ref, ids_hbm, weights_hbm, out_ref, ident_ref, ids_ref, weights_ref, both, arrived, *, exp_dev, per_group
):
    copies = [
        pltpu.make_async_copy(ids_hbm, ids_ref, arrived.at[0]),
        pltpu.make_async_copy(weights_hbm, weights_ref, arrived.at[1]),
    ]
    for copy in copies:
        copy.start()
    for copy in copies:
        copy.wait()
    top, count = ids_ref.shape
    chips = out_ref.shape[0]
    gap = 2 * exp_dev
    second = both.shape[0] // 2
    ids = ids_ref[...]
    chip = jnp.where(ids < 2 * per_group, lax.div(lax.rem(ids, per_group), exp_dev), -1)
    both[...] = jnp.zeros_like(both)
    both[0:top, :] = ids.astype(jnp.float32)
    both[second : second + top, :] = weights_ref[...]
    columns = both[...].T
    chip_lines = lax.broadcasted_iota(jnp.int32, (chips, count), 0)
    lanes = lax.broadcasted_iota(jnp.int32, (count, 128), 1)
    token = (lax.broadcasted_iota(jnp.int32, (count, 128), 0) + 1).astype(jnp.float32)
    total = jnp.zeros((chips, 128), jnp.float32)
    ident = jnp.zeros((count, 1), jnp.float32)
    for k in range(top):
        names = columns[:, k : k + 1].astype(jnp.int32)
        ident += jnp.where(names < 2 * per_group, 0.0, columns[:, second + k : second + k + 1])
        place = jnp.where(lax.div(names, per_group) == group_ref[0], 0, exp_dev) + lax.rem(names, exp_dev)
        high, middle, low = halves(columns[:, second + k : second + k + 1])
        value = jnp.where(lanes == place, token, 0.0)
        value = jnp.where(lanes == place + gap, high.astype(jnp.float32), value)
        value = jnp.where(lanes == place + 2 * gap, middle.astype(jnp.float32), value)
        value = jnp.where(lanes == place + 3 * gap, low, value)
        where = (chip_lines == chip[k : k + 1, :]).astype(jnp.float32).astype(jnp.bfloat16)
        total += mul(where, value.astype(jnp.bfloat16))
    ident_ref[...] = jnp.broadcast_to(ident, ident_ref.shape)
    weight = total + pltpu.roll(total, 128 - gap, 1) + pltpu.roll(total, 128 - 2 * gap, 1)
    lanes = lax.broadcasted_iota(jnp.int32, total.shape, 1)
    out_ref[...] = jnp.where(lanes < gap, total, jnp.where(lanes < 2 * gap, weight, 0.0))


def ask(group, ids, weights, chips, exp_dev, per_group):
    top, count = ids.shape
    vmem = pl.BlockSpec(memory_space=pltpu.VMEM)
    hbm = pl.BlockSpec(memory_space=pl.ANY)
    return pl.pallas_call(
        functools.partial(ask_kernel, exp_dev=exp_dev, per_group=per_group),
        out_shape=(
            jax.ShapeDtypeStruct((chips, 128), jnp.float32),
            jax.ShapeDtypeStruct((count, 128), jnp.float32),
        ),
        in_specs=[pl.BlockSpec(memory_space=pltpu.SMEM), hbm, hbm],
        out_specs=(vmem, vmem),
        scratch_shapes=[
            pltpu.VMEM((top, count), jnp.int32),
            pltpu.VMEM((top, count), jnp.float32),
            pltpu.VMEM((2 * (-(-top // 8) * 8), count), jnp.float32),
            pltpu.SemaphoreType.DMA((2,)),
        ],
        compiler_params=pltpu.CompilerParams(vmem_limit_bytes=MIX_VMEM),
        name="ask",
    )(group, in_hbm(ids), in_hbm(weights))


def pick_kernel(group_ref, chosen_ref, home_ref, lane_ref, own_ref, taken_ref, out_ref, held, arrived):
    sides, steps, exp_dev, capacity, block = held.shape
    start = pl.multiple_of(group_ref[0] * steps * block, block)
    copies = {}
    for i in range(steps):
        for side, ref in enumerate((own_ref, taken_ref)):
            copies[i, side] = pltpu.make_async_copy(
                ref.at[:, :, pl.ds(start + i * block, block)], held.at[side, i], arrived.at[side, i]
            )
            copies[i, side].start()

    chosen = chosen_ref[...]
    count = home_ref.shape[0]
    gap = sides * exp_dev
    homes = lax.broadcasted_iota(jnp.int32, (count, chosen.shape[0]), 1)
    earlier = (homes < home_ref[...]).astype(jnp.float32).astype(jnp.bfloat16)
    before = mul(earlier, (chosen > 0).astype(jnp.float32).astype(jnp.bfloat16))
    high, middle, low = halves(chosen)
    home_lanes = lax.broadcasted_iota(jnp.int32, chosen.shape, 1)
    packed = jnp.where(home_lanes < 4 * gap, pltpu.roll(middle.astype(jnp.float32), 2 * gap, 1), pltpu.roll(low, 4 * gap, 1))
    packed = jnp.where(home_lanes < 2 * gap, high.astype(jnp.float32), packed)
    this = (homes == home_ref[...]).astype(jnp.float32).astype(jnp.bfloat16)
    here = mul(this, packed.astype(jnp.bfloat16))
    lanes = lax.broadcasted_iota(jnp.int32, here.shape, 1)
    mine = lanes == lane_ref[...]
    token = jnp.sum(jnp.where(mine, here, 0.0), axis=1, keepdims=True)
    parts = (lax.rem(lanes, 2 * gap) == lane_ref[...] + gap) & (lanes < 6 * gap)
    weight = jnp.sum(jnp.where(parts, here, 0.0), axis=1, keepdims=True)
    rank = jnp.sum(jnp.where(mine, before, 0.0), axis=1, keepdims=True)
    code = jnp.where(token > 0, rank.astype(jnp.int32) + capacity * lax.rem(lane_ref[...], exp_dev), -1)
    slot = lax.broadcasted_iota(jnp.int32, (count, exp_dev * capacity), 1)
    select = (code == slot).astype(jnp.float32).astype(jnp.bfloat16)

    targets, lines, group = out_ref.shape
    each = count // sides
    rows = each // targets
    lanes = lanes[:each]
    note = jnp.where(lanes == 0, token[:each], jnp.where(lanes == 1, weight[:each], 0.0))
    note = jnp.where(lanes == 2, token[each:], jnp.where(lanes == 3, weight[each:], note))
    out_ref[:, lines - rows :, :] = note.reshape(targets, rows, group)
    per = block // group
    for i in range(steps):
        for side in range(sides):
            copies[i, side].wait()
            high, middle, _ = halves(held[side, i].reshape(exp_dev * capacity, block))
            wanted = select[side * each : (side + 1) * each, :]
            value = mul(wanted, high) + mul(wanted, middle)
            for j in range(per):
                line = ((i * per + j) * sides + side) * rows
                out_ref[:, line : line + rows, :] = value[:, j * group : (j + 1) * group].reshape(targets, rows, group)


def pick(group, chosen, home, lane, own, taken, targets):
    exp_dev, capacity, width = own.shape
    half = width // 2
    steps = half // BLOCK
    count = home.shape[0]
    slots = exp_dev * capacity
    lines = count // targets * half // 128 + count // targets // 2
    vmem = pl.BlockSpec(memory_space=pltpu.VMEM)
    hbm = pl.BlockSpec(memory_space=pl.ANY)
    return pl.pallas_call(
        pick_kernel,
        out_shape=jax.ShapeDtypeStruct((targets, lines, 128), jnp.float32),
        in_specs=[pl.BlockSpec(memory_space=pltpu.SMEM), vmem, vmem, vmem, hbm, hbm],
        out_specs=vmem,
        scratch_shapes=[
            pltpu.VMEM((2, steps, exp_dev, capacity, BLOCK), jnp.float32),
            pltpu.SemaphoreType.DMA((2, steps)),
        ],
        compiler_params=pltpu.CompilerParams(vmem_limit_bytes=PICK_VMEM),
        cost_estimate=pl.CostEstimate(
            flops=4 * count * slots * half, bytes_accessed=4 * (2 * slots + count) * half, transcendentals=0
        ),
        name="pick",
    )(group, chosen, home, lane, own, taken)


def mixed(rows_ref, tok_dev, exp_dev, offsets):
    far = 4
    sources, lines, group = rows_ref.shape
    rows = far * exp_dev
    count = len(offsets) * tok_dev
    note = rows_ref[:, lines - rows :, :].reshape(sources * rows, group)
    line = lax.broadcasted_iota(jnp.int32, (sources * rows, count), 0)
    out_line = lax.broadcasted_iota(jnp.int32, (sources * rows, count), 1)
    fits = lax.div(lax.rem(line, rows), exp_dev) == lax.div(out_line, tok_dev) + offsets[0]
    token = jnp.where(fits, lax.rem(out_line, tok_dev) + 1, -1).astype(jnp.float32)
    sides = []
    for side in range(2):
        named = note[:, 2 * side : 2 * side + 1] == token
        mix = jnp.where(named, note[:, 2 * side + 1 : 2 * side + 2], 0.0)
        sides.append(mix.reshape(sources, rows, count))
    mix = jnp.concatenate(sides, axis=1).reshape(2 * sources * rows, count).T
    m_high, m_middle, _ = halves(mix)
    both = jnp.concatenate([m_high, m_middle], axis=0)
    per = BLOCK // group
    for i in range((lines - rows) // (2 * rows * per)):
        parts = [rows_ref[:, 2 * rows * (i * per + j) : 2 * rows * (i * per + j + 1), :] for j in range(per)]
        block = jnp.concatenate([part.reshape(2 * sources * rows, group) for part in parts], axis=1)
        high, middle, _ = halves(block)
        value = mul(both, high)
        value = value[:count] + (value[count:] + mul(m_high, middle))
        yield i, [value[o * tok_dev : (o + 1) * tok_dev] for o in range(len(offsets))]


def combine_kernel(rows_ref, far_up, far_down, near_left, near_right, prev_left, prev_right, *, exp_dev):
    tok_dev, cut = far_up.shape
    for i, (nxt, opposite, prev) in mixed(rows_ref, tok_dev, exp_dev, (1, 2, 3)):
        first = i * BLOCK < cut
        here = slice(i * BLOCK % cut, i * BLOCK % cut + BLOCK)
        (far_up if first else far_down)[:, here] = opposite
        (near_left if first else near_right)[:, here] = nxt
        (prev_left if first else prev_right)[:, here] = prev


def own_kernel(group_ref, rows_ref, ident_ref, tokens_ref, base_ref, own, arrived, *, exp_dev):
    tok_dev, half = base_ref.shape
    copy = pltpu.make_async_copy(
        tokens_ref.at[:, pl.ds(pl.multiple_of(group_ref[0] * half, half), half)], own, arrived
    )
    copy.start()
    copy.wait()
    for i, (near,) in mixed(rows_ref, tok_dev, exp_dev, (0,)):
        here = slice(i * BLOCK, (i + 1) * BLOCK)
        base_ref[:, here] = near + ident_ref[:, 0:1] * own[:, here]


def cost(offsets, tok_dev, rows, half):
    depth = rows.shape[0] * (rows.shape[1] * 128 // half)
    return pl.CostEstimate(
        flops=6 * offsets * tok_dev * depth * half, bytes_accessed=4 * depth * half, transcendentals=0
    )


def combine(rows, tok_dev, half, exp_dev):
    vmem = pl.BlockSpec(memory_space=pltpu.VMEM)
    return pl.pallas_call(
        functools.partial(combine_kernel, exp_dev=exp_dev),
        out_shape=[jax.ShapeDtypeStruct((tok_dev, half // 2), jnp.float32)] * 6,
        in_specs=[vmem],
        out_specs=[vmem] * 6,
        compiler_params=pltpu.CompilerParams(vmem_limit_bytes=MIX_VMEM),
        cost_estimate=cost(3, tok_dev, rows, half),
        name="combine",
    )(rows)


def own_sum(group, rows, ident, tokens, exp_dev):
    tok_dev, width = tokens.shape
    half = width // 2
    vmem = pl.BlockSpec(memory_space=pltpu.VMEM)
    return pl.pallas_call(
        functools.partial(own_kernel, exp_dev=exp_dev),
        out_shape=jax.ShapeDtypeStruct((tok_dev, half), jnp.float32),
        in_specs=[pl.BlockSpec(memory_space=pltpu.SMEM), vmem, vmem, pl.BlockSpec(memory_space=pl.ANY)],
        out_specs=vmem,
        scratch_shapes=[pltpu.VMEM((tok_dev, half), jnp.float32), pltpu.SemaphoreType.DMA],
        compiler_params=pltpu.CompilerParams(vmem_limit_bytes=MIX_VMEM),
        cost_estimate=cost(1, tok_dev, rows, half),
        name="own_sum",
    )(group, rows, ident, in_hbm(tokens))


def finish_kernel(base_ref, left_ref, more_left_ref, right_ref, more_right_ref, out_ref):
    _, cut = left_ref.shape
    out_ref[:, :cut] = base_ref[:, :cut] + more_left_ref[...] + left_ref[...]
    out_ref[:, cut:] = base_ref[:, cut:] + more_right_ref[...] + right_ref[...]


def finish(base, *parts):
    vmem = pl.BlockSpec(memory_space=pltpu.VMEM)
    return pl.pallas_call(
        finish_kernel,
        out_shape=jax.ShapeDtypeStruct(base.shape, jnp.float32),
        in_specs=[vmem] * 5,
        out_specs=vmem,
        compiler_params=pltpu.CompilerParams(vmem_limit_bytes=MIX_VMEM),
        name="finish",
    )(base, *parts)


def shift(count, by):
    return [(i, (i + by) % count) for i in range(count)]


def shards(tokens, route_ids, route_weights, expert_rows):
    group = lax.axis_index("grp")
    ep_count = lax.axis_size(EP)
    far = lax.axis_size("zh")
    low = lax.axis_size("zl")
    near = ep_count // far
    tok_dev, top = route_ids.shape
    exp_dev, capacity, width = expert_rows.shape
    half = width // 2
    held = 2 * exp_dev
    per_group = exp_dev * ep_count
    experts = 2 * per_group

    taken = lax.ppermute(expert_rows, "grp", [(0, 1), (1, 0)])

    group_word = group.astype(jnp.int32).reshape(1)
    asked, ident = ask(group_word, route_ids.T, route_weights.T, ep_count, exp_dev, per_group)
    chosen = lax.all_to_all(asked[:, None, :], EP, 0, 0, tiled=True).reshape(ep_count, 128)

    row = jnp.arange(ep_count * held, dtype=jnp.int32)[:, None]
    r_side = row // (ep_count * exp_dev)
    r_near = row % (ep_count * exp_dev) // (far * exp_dev)
    r_far = row % (far * exp_dev) // exp_dev
    r_exp = row % exp_dev
    zh = lax.axis_index("zh")
    home = (r_near // low * far + (zh + r_far) % far) * low + r_near % low
    lane = r_side * exp_dev + r_exp

    chosen, home, lane, taken = lax.optimization_barrier((chosen, home, lane, taken))
    outgoing = pick(group_word, chosen, home, lane, in_hbm(expert_rows), taken, near)

    rows = lax.all_to_all(outgoing, NEAR, 0, 0, tiled=True)
    up, down = shift(far, 1), shift(far, -1)
    far_up, far_down, near_left, near_right, prev_left, prev_right = combine(rows, tok_dev, half, exp_dev)
    far_up, far_down = lax.ppermute(far_up, "zh", up), lax.ppermute(far_down, "zh", down)
    more_right, more_left = lax.ppermute(near_right, "zh", up), lax.ppermute(prev_left, "zh", down)
    base = own_sum(group_word, rows, ident, tokens, exp_dev)
    left = lax.ppermute(near_left + far_up, "zh", up)
    right = lax.ppermute(prev_right + far_down, "zh", down)
    return finish(base, left, more_left, right, more_right)


def solution(mesh):
    torus = Mesh(mesh.devices.reshape(mesh.shape["grp"], 4, 4, 4, 2), ("grp",) + EP)
    in_specs = (P(EP, None), P(EP, None), P(EP, None), P(("grp",) + EP, None, None))
    return jax.shard_map(
        shards, mesh=torus, in_specs=in_specs, out_specs=P(EP, "grp"), check_vma=False
    )
```

```python
import functools

import jax
import jax.numpy as jnp
from jax import lax
from jax.sharding import Mesh
from jax.sharding import PartitionSpec as P
from jax.experimental import pallas as pl
from jax.experimental.pallas import tpu as pltpu

EP = ("x", "y", "zh", "zl")
NEAR = ("x", "y", "zl")
BLOCK = 512
PICK_VMEM = 24 * 1024 * 1024
MIX_VMEM = 24 * 1024 * 1024


def halves(x):
    high = x.astype(jnp.bfloat16)
    rest = x - high.astype(jnp.float32)
    middle = rest.astype(jnp.bfloat16)
    return high, middle, rest - middle.astype(jnp.float32)


def in_hbm(x):
    return pltpu.with_memory_space_constraint(x, pltpu.HBM)


def mul(a, b):
    return jnp.dot(a, b, preferred_element_type=jnp.float32)


def ask_kernel(
    group_ref, ids_hbm, weights_hbm, out_ref, ident_ref, ids_ref, weights_ref, both, arrived, *, exp_dev, per_group
):
    copies = [
        pltpu.make_async_copy(ids_hbm, ids_ref, arrived.at[0]),
        pltpu.make_async_copy(weights_hbm, weights_ref, arrived.at[1]),
    ]
    for copy in copies:
        copy.start()
    for copy in copies:
        copy.wait()
    top, count = ids_ref.shape
    chips = out_ref.shape[0]
    gap = 2 * exp_dev
    second = both.shape[0] // 2
    ids = ids_ref[...]
    chip = jnp.where(ids < 2 * per_group, lax.div(lax.rem(ids, per_group), exp_dev), -1)
    both[...] = jnp.zeros_like(both)
    both[0:top, :] = ids.astype(jnp.float32)
    both[second : second + top, :] = weights_ref[...]
    columns = both[...].T
    chip_lines = lax.broadcasted_iota(jnp.int32, (chips, count), 0)
    lanes = lax.broadcasted_iota(jnp.int32, (count, 128), 1)
    token = (lax.broadcasted_iota(jnp.int32, (count, 128), 0) + 1).astype(jnp.float32)
    total = jnp.zeros((chips, 128), jnp.float32)
    ident = jnp.zeros((count, 1), jnp.float32)
    for k in range(top):
        names = columns[:, k : k + 1].astype(jnp.int32)
        ident += jnp.where(names < 2 * per_group, 0.0, columns[:, second + k : second + k + 1])
        place = jnp.where(lax.div(names, per_group) == group_ref[0], 0, exp_dev) + lax.rem(names, exp_dev)
        high, middle, low = halves(columns[:, second + k : second + k + 1])
        value = jnp.where(lanes == place, token, 0.0)
        value = jnp.where(lanes == place + gap, high.astype(jnp.float32), value)
        value = jnp.where(lanes == place + 2 * gap, middle.astype(jnp.float32), value)
        value = jnp.where(lanes == place + 3 * gap, low, value)
        where = (chip_lines == chip[k : k + 1, :]).astype(jnp.float32).astype(jnp.bfloat16)
        total += mul(where, value.astype(jnp.bfloat16))
    ident_ref[...] = jnp.broadcast_to(ident, ident_ref.shape)
    weight = total + pltpu.roll(total, 128 - gap, 1) + pltpu.roll(total, 128 - 2 * gap, 1)
    lanes = lax.broadcasted_iota(jnp.int32, total.shape, 1)
    out_ref[...] = jnp.where(lanes < gap, total, jnp.where(lanes < 2 * gap, weight, 0.0))


def ask(group, ids, weights, chips, exp_dev, per_group):
    top, count = ids.shape
    vmem = pl.BlockSpec(memory_space=pltpu.VMEM)
    hbm = pl.BlockSpec(memory_space=pl.ANY)
    return pl.pallas_call(
        functools.partial(ask_kernel, exp_dev=exp_dev, per_group=per_group),
        out_shape=(
            jax.ShapeDtypeStruct((chips, 128), jnp.float32),
            jax.ShapeDtypeStruct((count, 128), jnp.float32),
        ),
        in_specs=[pl.BlockSpec(memory_space=pltpu.SMEM), hbm, hbm],
        out_specs=(vmem, vmem),
        scratch_shapes=[
            pltpu.VMEM((top, count), jnp.int32),
            pltpu.VMEM((top, count), jnp.float32),
            pltpu.VMEM((2 * (-(-top // 8) * 8), count), jnp.float32),
            pltpu.SemaphoreType.DMA((2,)),
        ],
        compiler_params=pltpu.CompilerParams(vmem_limit_bytes=MIX_VMEM),
        name="ask",
    )(group, in_hbm(ids), in_hbm(weights))


def pick_kernel(group_ref, chosen_ref, home_ref, lane_ref, own_ref, taken_ref, out_ref, held, arrived):
    sides, steps, exp_dev, capacity, block = held.shape
    start = pl.multiple_of(group_ref[0] * steps * block, block)
    copies = {}
    for i in range(steps):
        for side, ref in enumerate((own_ref, taken_ref)):
            copies[i, side] = pltpu.make_async_copy(
                ref.at[:, :, pl.ds(start + i * block, block)], held.at[side, i], arrived.at[side, i]
            )
            copies[i, side].start()

    chosen = chosen_ref[...]
    count = home_ref.shape[0]
    gap = sides * exp_dev
    homes = lax.broadcasted_iota(jnp.int32, (count, chosen.shape[0]), 1)
    earlier = (homes < home_ref[...]).astype(jnp.float32).astype(jnp.bfloat16)
    before = mul(earlier, (chosen > 0).astype(jnp.float32).astype(jnp.bfloat16))
    high, middle, low = halves(chosen)
    home_lanes = lax.broadcasted_iota(jnp.int32, chosen.shape, 1)
    packed = jnp.where(home_lanes < 4 * gap, pltpu.roll(middle.astype(jnp.float32), 2 * gap, 1), pltpu.roll(low, 4 * gap, 1))
    packed = jnp.where(home_lanes < 2 * gap, high.astype(jnp.float32), packed)
    this = (homes == home_ref[...]).astype(jnp.float32).astype(jnp.bfloat16)
    here = mul(this, packed.astype(jnp.bfloat16))
    lanes = lax.broadcasted_iota(jnp.int32, here.shape, 1)
    mine = lanes == lane_ref[...]
    token = jnp.sum(jnp.where(mine, here, 0.0), axis=1, keepdims=True)
    parts = (lax.rem(lanes, 2 * gap) == lane_ref[...] + gap) & (lanes < 6 * gap)
    weight = jnp.sum(jnp.where(parts, here, 0.0), axis=1, keepdims=True)
    rank = jnp.sum(jnp.where(mine, before, 0.0), axis=1, keepdims=True)
    code = jnp.where(token > 0, rank.astype(jnp.int32) + capacity * lax.rem(lane_ref[...], exp_dev), -1)
    slot = lax.broadcasted_iota(jnp.int32, (count, exp_dev * capacity), 1)
    select = (code == slot).astype(jnp.float32).astype(jnp.bfloat16)

    targets, lines, group = out_ref.shape
    each = count // sides
    rows = each // targets
    lanes = lanes[:each]
    note = jnp.where(lanes == 0, token[:each], jnp.where(lanes == 1, weight[:each], 0.0))
    note = jnp.where(lanes == 2, token[each:], jnp.where(lanes == 3, weight[each:], note))
    out_ref[:, lines - rows :, :] = note.reshape(targets, rows, group)
    per = block // group
    for i in range(steps):
        for side in range(sides):
            copies[i, side].wait()
            high, middle, _ = halves(held[side, i].reshape(exp_dev * capacity, block))
            wanted = select[side * each : (side + 1) * each, :]
            value = mul(wanted, high) + mul(wanted, middle)
            for j in range(per):
                line = ((i * per + j) * sides + side) * rows
                out_ref[:, line : line + rows, :] = value[:, j * group : (j + 1) * group].reshape(targets, rows, group)


def pick(group, chosen, home, lane, own, taken, targets):
    exp_dev, capacity, width = own.shape
    half = width // 2
    steps = half // BLOCK
    count = home.shape[0]
    slots = exp_dev * capacity
    lines = count // targets * half // 128 + count // targets // 2
    vmem = pl.BlockSpec(memory_space=pltpu.VMEM)
    hbm = pl.BlockSpec(memory_space=pl.ANY)
    return pl.pallas_call(
        pick_kernel,
        out_shape=jax.ShapeDtypeStruct((targets, lines, 128), jnp.float32),
        in_specs=[pl.BlockSpec(memory_space=pltpu.SMEM), vmem, vmem, vmem, hbm, hbm],
        out_specs=vmem,
        scratch_shapes=[
            pltpu.VMEM((2, steps, exp_dev, capacity, BLOCK), jnp.float32),
            pltpu.SemaphoreType.DMA((2, steps)),
        ],
        compiler_params=pltpu.CompilerParams(vmem_limit_bytes=PICK_VMEM),
        cost_estimate=pl.CostEstimate(
            flops=4 * count * slots * half, bytes_accessed=4 * (2 * slots + count) * half, transcendentals=0
        ),
        name="pick",
    )(group, chosen, home, lane, own, taken)


def mixed(rows_ref, tok_dev, exp_dev, offsets):
    far = 4
    sources, lines, group = rows_ref.shape
    rows = far * exp_dev
    count = len(offsets) * tok_dev
    note = rows_ref[:, lines - rows :, :].reshape(sources * rows, group)
    line = lax.broadcasted_iota(jnp.int32, (sources * rows, count), 0)
    out_line = lax.broadcasted_iota(jnp.int32, (sources * rows, count), 1)
    fits = lax.div(lax.rem(line, rows), exp_dev) == lax.rem(lax.div(out_line, tok_dev) + offsets[0], far)
    token = jnp.where(fits, lax.rem(out_line, tok_dev) + 1, -1).astype(jnp.float32)
    sides = []
    for side in range(2):
        named = note[:, 2 * side : 2 * side + 1] == token
        mix = jnp.where(named, note[:, 2 * side + 1 : 2 * side + 2], 0.0)
        sides.append(mix.reshape(sources, rows, count))
    mix = jnp.concatenate(sides, axis=1).reshape(2 * sources * rows, count).T
    m_high, m_middle, _ = halves(mix)
    both = jnp.concatenate([m_high, m_middle], axis=0)
    per = BLOCK // group
    for i in range((lines - rows) // (2 * rows * per)):
        parts = [rows_ref[:, 2 * rows * (i * per + j) : 2 * rows * (i * per + j + 1), :] for j in range(per)]
        block = jnp.concatenate([part.reshape(2 * sources * rows, group) for part in parts], axis=1)
        high, middle, _ = halves(block)
        value = mul(both, high)
        value = value[:count] + (value[count:] + mul(m_high, middle))
        yield i, [value[o * tok_dev : (o + 1) * tok_dev] for o in range(len(offsets))]


def far_kernel(rows_ref, up_ref, down_ref, *, exp_dev):
    tok_dev, cut = up_ref.shape
    for i, (opposite,) in mixed(rows_ref, tok_dev, exp_dev, (2,)):
        here = slice(i * BLOCK % cut, i * BLOCK % cut + BLOCK)
        (up_ref if i * BLOCK < cut else down_ref)[:, here] = opposite


def rest_kernel(
    group_ref, rows_ref, ident_ref, tokens_ref, base_ref, near_left, near_right, prev_left, prev_right, own, arrived, *, exp_dev
):
    tok_dev, half = base_ref.shape
    cut = half // 2
    copy = pltpu.make_async_copy(
        tokens_ref.at[:, pl.ds(pl.multiple_of(group_ref[0] * half, half), half)], own, arrived
    )
    copy.start()
    for i, (prev, home, nxt) in mixed(rows_ref, tok_dev, exp_dev, (3, 0, 1)):
        if i == 0:
            copy.wait()
        here = slice(i * BLOCK, (i + 1) * BLOCK)
        base_ref[:, here] = home + ident_ref[:, 0:1] * own[:, here]
        first = i * BLOCK < cut
        here = slice(i * BLOCK % cut, i * BLOCK % cut + BLOCK)
        (near_left if first else near_right)[:, here] = nxt
        (prev_left if first else prev_right)[:, here] = prev


def cost(offsets, tok_dev, rows, half):
    depth = rows.shape[0] * (rows.shape[1] * 128 // half)
    return pl.CostEstimate(
        flops=6 * offsets * tok_dev * depth * half, bytes_accessed=4 * depth * half, transcendentals=0
    )


def far_sum(rows, tok_dev, half, exp_dev):
    vmem = pl.BlockSpec(memory_space=pltpu.VMEM)
    return pl.pallas_call(
        functools.partial(far_kernel, exp_dev=exp_dev),
        out_shape=[jax.ShapeDtypeStruct((tok_dev, half // 2), jnp.float32)] * 2,
        in_specs=[vmem],
        out_specs=[vmem] * 2,
        compiler_params=pltpu.CompilerParams(vmem_limit_bytes=MIX_VMEM),
        cost_estimate=cost(1, tok_dev, rows, half),
        name="far_sum",
    )(rows)


def rest_sum(group, rows, ident, tokens, exp_dev):
    tok_dev, width = tokens.shape
    half = width // 2
    vmem = pl.BlockSpec(memory_space=pltpu.VMEM)
    return pl.pallas_call(
        functools.partial(rest_kernel, exp_dev=exp_dev),
        out_shape=[jax.ShapeDtypeStruct((tok_dev, half), jnp.float32)]
        + [jax.ShapeDtypeStruct((tok_dev, half // 2), jnp.float32)] * 4,
        in_specs=[pl.BlockSpec(memory_space=pltpu.SMEM), vmem, vmem, pl.BlockSpec(memory_space=pl.ANY)],
        out_specs=[vmem] * 5,
        scratch_shapes=[pltpu.VMEM((tok_dev, half), jnp.float32), pltpu.SemaphoreType.DMA],
        compiler_params=pltpu.CompilerParams(vmem_limit_bytes=MIX_VMEM),
        cost_estimate=cost(3, tok_dev, rows, half),
        name="rest_sum",
    )(group, rows, ident, in_hbm(tokens))


def finish_kernel(base_ref, left_ref, more_left_ref, right_ref, more_right_ref, out_ref):
    _, cut = left_ref.shape
    out_ref[:, :cut] = base_ref[:, :cut] + more_left_ref[...] + left_ref[...]
    out_ref[:, cut:] = base_ref[:, cut:] + more_right_ref[...] + right_ref[...]


def finish(base, *parts):
    vmem = pl.BlockSpec(memory_space=pltpu.VMEM)
    return pl.pallas_call(
        finish_kernel,
        out_shape=jax.ShapeDtypeStruct(base.shape, jnp.float32),
        in_specs=[vmem] * 5,
        out_specs=vmem,
        compiler_params=pltpu.CompilerParams(vmem_limit_bytes=MIX_VMEM),
        name="finish",
    )(base, *parts)


def shift(count, by):
    return [(i, (i + by) % count) for i in range(count)]


def shards(tokens, route_ids, route_weights, expert_rows):
    group = lax.axis_index("grp")
    ep_count = lax.axis_size(EP)
    far = lax.axis_size("zh")
    low = lax.axis_size("zl")
    near = ep_count // far
    tok_dev, top = route_ids.shape
    exp_dev, capacity, width = expert_rows.shape
    half = width // 2
    held = 2 * exp_dev
    per_group = exp_dev * ep_count
    experts = 2 * per_group

    taken = lax.ppermute(expert_rows, "grp", [(0, 1), (1, 0)])

    group_word = group.astype(jnp.int32).reshape(1)
    asked, ident = ask(group_word, route_ids.T, route_weights.T, ep_count, exp_dev, per_group)
    chosen = lax.all_to_all(asked[:, None, :], EP, 0, 0, tiled=True).reshape(ep_count, 128)

    row = jnp.arange(ep_count * held, dtype=jnp.int32)[:, None]
    r_side = row // (ep_count * exp_dev)
    r_near = row % (ep_count * exp_dev) // (far * exp_dev)
    r_far = row % (far * exp_dev) // exp_dev
    r_exp = row % exp_dev
    zh = lax.axis_index("zh")
    home = (r_near // low * far + (zh + r_far) % far) * low + r_near % low
    lane = r_side * exp_dev + r_exp

    chosen, home, lane, taken = lax.optimization_barrier((chosen, home, lane, taken))
    outgoing = pick(group_word, chosen, home, lane, in_hbm(expert_rows), taken, near)

    rows = lax.all_to_all(outgoing, NEAR, 0, 0, tiled=True)
    up, down = shift(far, 1), shift(far, -1)
    far_up, far_down = far_sum(rows, tok_dev, half, exp_dev)
    rows, far_up, far_down = lax.optimization_barrier((rows, far_up, far_down))
    far_up, far_down = lax.ppermute(far_up, "zh", up), lax.ppermute(far_down, "zh", down)
    base, near_left, near_right, prev_left, prev_right = rest_sum(group_word, rows, ident, tokens, exp_dev)
    more_right, more_left = lax.ppermute(near_right, "zh", up), lax.ppermute(prev_left, "zh", down)
    left = lax.ppermute(near_left + far_up, "zh", up)
    right = lax.ppermute(prev_right + far_down, "zh", down)
    return finish(base, left, more_left, right, more_right)


def solution(mesh):
    torus = Mesh(mesh.devices.reshape(mesh.shape["grp"], 4, 4, 4, 2), ("grp",) + EP)
    in_specs = (P(EP, None), P(EP, None), P(EP, None), P(("grp",) + EP, None, None))
    return jax.shard_map(
        shards, mesh=torus, in_specs=in_specs, out_specs=P(EP, "grp"), check_vma=False
    )
```

```python
import functools

import jax
import jax.numpy as jnp
from jax import lax
from jax.sharding import Mesh
from jax.sharding import PartitionSpec as P
from jax.experimental import pallas as pl
from jax.experimental.pallas import tpu as pltpu

EP = ("x", "y", "zh", "zl")
NEAR = ("x", "y", "zl")
BLOCK = 512
PICK_BLOCK = 1024
PICK_VMEM = 24 * 1024 * 1024
MIX_VMEM = 24 * 1024 * 1024


def halves(x):
    high = x.astype(jnp.bfloat16)
    rest = x - high.astype(jnp.float32)
    middle = rest.astype(jnp.bfloat16)
    return high, middle, rest - middle.astype(jnp.float32)


def in_hbm(x):
    return pltpu.with_memory_space_constraint(x, pltpu.HBM)


def mul(a, b):
    return jnp.dot(a, b, preferred_element_type=jnp.float32)


def ask_kernel(
    group_ref, ids_hbm, weights_hbm, out_ref, ident_ref, ids_ref, weights_ref, both, arrived, *, exp_dev, per_group
):
    copies = [
        pltpu.make_async_copy(ids_hbm, ids_ref, arrived.at[0]),
        pltpu.make_async_copy(weights_hbm, weights_ref, arrived.at[1]),
    ]
    for copy in copies:
        copy.start()
    for copy in copies:
        copy.wait()
    top, count = ids_ref.shape
    chips = out_ref.shape[0]
    gap = 2 * exp_dev
    second = both.shape[0] // 2
    ids = ids_ref[...]
    chip = jnp.where(ids < 2 * per_group, lax.div(lax.rem(ids, per_group), exp_dev), -1)
    both[...] = jnp.zeros_like(both)
    both[0:top, :] = ids.astype(jnp.float32)
    both[second : second + top, :] = weights_ref[...]
    columns = both[...].T
    together = 128 // count
    chip_lines = lax.broadcasted_iota(jnp.int32, (chips, 128), 0)
    values = []
    lanes = lax.broadcasted_iota(jnp.int32, (count, 128), 1)
    token = (lax.broadcasted_iota(jnp.int32, (count, 128), 0) + 1).astype(jnp.float32)
    total = jnp.zeros((chips, 128), jnp.float32)
    ident = jnp.zeros((count, 1), jnp.float32)
    for k in range(top):
        names = columns[:, k : k + 1].astype(jnp.int32)
        ident += jnp.where(names < 2 * per_group, 0.0, columns[:, second + k : second + k + 1])
        place = jnp.where(lax.div(names, per_group) == group_ref[0], 0, exp_dev) + lax.rem(names, exp_dev)
        high, middle, low = halves(columns[:, second + k : second + k + 1])
        value = jnp.where(lanes == place, token, 0.0)
        value = jnp.where(lanes == place + gap, high.astype(jnp.float32), value)
        value = jnp.where(lanes == place + 2 * gap, middle.astype(jnp.float32), value)
        value = jnp.where(lanes == place + 3 * gap, low, value)
        values.append(value)
        if len(values) == together:
            names = jnp.concatenate([chip[j : j + 1, :] for j in range(k + 1 - together, k + 1)], axis=1)
            where = (chip_lines == names).astype(jnp.float32).astype(jnp.bfloat16)
            total += mul(where, jnp.concatenate(values, axis=0).astype(jnp.bfloat16))
            values = []
    ident_ref[...] = jnp.broadcast_to(ident, ident_ref.shape)
    weight = total + pltpu.roll(total, 128 - gap, 1) + pltpu.roll(total, 128 - 2 * gap, 1)
    lanes = lax.broadcasted_iota(jnp.int32, total.shape, 1)
    out_ref[...] = jnp.where(lanes < gap, total, jnp.where(lanes < 2 * gap, weight, 0.0))


def ask(group, ids, weights, chips, exp_dev, per_group):
    top, count = ids.shape
    vmem = pl.BlockSpec(memory_space=pltpu.VMEM)
    hbm = pl.BlockSpec(memory_space=pl.ANY)
    return pl.pallas_call(
        functools.partial(ask_kernel, exp_dev=exp_dev, per_group=per_group),
        out_shape=(
            jax.ShapeDtypeStruct((chips, 128), jnp.float32),
            jax.ShapeDtypeStruct((count, 128), jnp.float32),
        ),
        in_specs=[pl.BlockSpec(memory_space=pltpu.SMEM), hbm, hbm],
        out_specs=(vmem, vmem),
        scratch_shapes=[
            pltpu.VMEM((top, count), jnp.int32),
            pltpu.VMEM((top, count), jnp.float32),
            pltpu.VMEM((2 * (-(-top // 8) * 8), count), jnp.float32),
            pltpu.SemaphoreType.DMA((2,)),
        ],
        compiler_params=pltpu.CompilerParams(vmem_limit_bytes=MIX_VMEM),
        name="ask",
    )(group, in_hbm(ids), in_hbm(weights))


def pick_kernel(group_ref, chosen_ref, home_ref, lane_ref, own_ref, taken_ref, out_ref, held, arrived):
    sides, steps, exp_dev, capacity, block = held.shape
    start = pl.multiple_of(group_ref[0] * steps * block, block)
    copies = {}
    for i in range(steps):
        for side, ref in enumerate((own_ref, taken_ref)):
            copies[i, side] = pltpu.make_async_copy(
                ref.at[:, :, pl.ds(start + i * block, block)], held.at[side, i], arrived.at[side, i]
            )
            copies[i, side].start()

    chosen = chosen_ref[...]
    count = home_ref.shape[0]
    gap = sides * exp_dev
    homes = lax.broadcasted_iota(jnp.int32, (count, chosen.shape[0]), 1)
    earlier = (homes < home_ref[...]).astype(jnp.float32).astype(jnp.bfloat16)
    before = mul(earlier, (chosen > 0).astype(jnp.float32).astype(jnp.bfloat16))
    high, middle, low = halves(chosen)
    home_lanes = lax.broadcasted_iota(jnp.int32, chosen.shape, 1)
    packed = jnp.where(home_lanes < 4 * gap, pltpu.roll(middle.astype(jnp.float32), 2 * gap, 1), pltpu.roll(low, 4 * gap, 1))
    packed = jnp.where(home_lanes < 2 * gap, high.astype(jnp.float32), packed)
    this = (homes == home_ref[...]).astype(jnp.float32).astype(jnp.bfloat16)
    here = mul(this, packed.astype(jnp.bfloat16))
    lanes = lax.broadcasted_iota(jnp.int32, here.shape, 1)
    mine = lanes == lane_ref[...]
    token = jnp.sum(jnp.where(mine, here, 0.0), axis=1, keepdims=True)
    parts = (lax.rem(lanes, 2 * gap) == lane_ref[...] + gap) & (lanes < 6 * gap)
    weight = jnp.sum(jnp.where(parts, here, 0.0), axis=1, keepdims=True)
    rank = jnp.sum(jnp.where(mine, before, 0.0), axis=1, keepdims=True)
    code = jnp.where(token > 0, rank.astype(jnp.int32) + capacity * lax.rem(lane_ref[...], exp_dev), -1)
    slot = lax.broadcasted_iota(jnp.int32, (count, exp_dev * capacity), 1)
    select = (code == slot).astype(jnp.float32).astype(jnp.bfloat16)

    targets, lines, group = out_ref.shape
    each = count // sides
    rows = each // targets
    lanes = lanes[:each]
    note = jnp.where(lanes == 0, token[:each], jnp.where(lanes == 1, weight[:each], 0.0))
    note = jnp.where(lanes == 2, token[each:], jnp.where(lanes == 3, weight[each:], note))
    out_ref[:, lines - rows :, :] = note.reshape(targets, rows, group)
    per = block // group
    for i in range(steps):
        for side in range(sides):
            copies[i, side].wait()
            high, middle, _ = halves(held[side, i].reshape(exp_dev * capacity, block))
            wanted = select[side * each : (side + 1) * each, :]
            value = mul(wanted, high) + mul(wanted, middle)
            for j in range(per):
                line = ((i * per + j) * sides + side) * rows
                out_ref[:, line : line + rows, :] = value[:, j * group : (j + 1) * group].reshape(targets, rows, group)


def pick(group, chosen, home, lane, own, taken, targets):
    exp_dev, capacity, width = own.shape
    half = width // 2
    steps = half // PICK_BLOCK
    count = home.shape[0]
    slots = exp_dev * capacity
    lines = count // targets * half // 128 + count // targets // 2
    vmem = pl.BlockSpec(memory_space=pltpu.VMEM)
    hbm = pl.BlockSpec(memory_space=pl.ANY)
    return pl.pallas_call(
        pick_kernel,
        out_shape=jax.ShapeDtypeStruct((targets, lines, 128), jnp.float32),
        in_specs=[pl.BlockSpec(memory_space=pltpu.SMEM), vmem, vmem, vmem, hbm, hbm],
        out_specs=vmem,
        scratch_shapes=[
            pltpu.VMEM((2, steps, exp_dev, capacity, PICK_BLOCK), jnp.float32),
            pltpu.SemaphoreType.DMA((2, steps)),
        ],
        compiler_params=pltpu.CompilerParams(vmem_limit_bytes=PICK_VMEM),
        cost_estimate=pl.CostEstimate(
            flops=4 * count * slots * half, bytes_accessed=4 * (2 * slots + count) * half, transcendentals=0
        ),
        name="pick",
    )(group, chosen, home, lane, own, taken)


def mixed(rows_ref, tok_dev, exp_dev, offsets):
    far = 4
    sources, lines, group = rows_ref.shape
    rows = far * exp_dev
    count = len(offsets) * tok_dev
    note = rows_ref[:, lines - rows :, :].reshape(sources * rows, group)
    line = lax.broadcasted_iota(jnp.int32, (sources * rows, count), 0)
    out_line = lax.broadcasted_iota(jnp.int32, (sources * rows, count), 1)
    fits = lax.div(lax.rem(line, rows), exp_dev) == lax.div(out_line, tok_dev) + offsets[0]
    token = jnp.where(fits, lax.rem(out_line, tok_dev) + 1, -1).astype(jnp.float32)
    sides = []
    for side in range(2):
        named = note[:, 2 * side : 2 * side + 1] == token
        mix = jnp.where(named, note[:, 2 * side + 1 : 2 * side + 2], 0.0)
        sides.append(mix.reshape(sources, rows, count))
    mix = jnp.concatenate(sides, axis=1).reshape(2 * sources * rows, count).T
    m_high, m_middle, _ = halves(mix)
    both = jnp.concatenate([m_high, m_middle], axis=0)
    per = BLOCK // group
    for i in range((lines - rows) // (2 * rows * per)):
        parts = [rows_ref[:, 2 * rows * (i * per + j) : 2 * rows * (i * per + j + 1), :] for j in range(per)]
        block = jnp.concatenate([part.reshape(2 * sources * rows, group) for part in parts], axis=1)
        high, middle, _ = halves(block)
        value = mul(both, high)
        value = value[:count] + (value[count:] + mul(m_high, middle))
        yield i, [value[o * tok_dev : (o + 1) * tok_dev] for o in range(len(offsets))]


def combine_kernel(rows_ref, far_up, far_down, near_left, near_right, prev_left, prev_right, *, exp_dev):
    tok_dev, cut = far_up.shape
    for i, (nxt, opposite, prev) in mixed(rows_ref, tok_dev, exp_dev, (1, 2, 3)):
        first = i * BLOCK < cut
        here = slice(i * BLOCK % cut, i * BLOCK % cut + BLOCK)
        (far_up if first else far_down)[:, here] = opposite
        (near_left if first else near_right)[:, here] = nxt
        (prev_left if first else prev_right)[:, here] = prev


def own_kernel(group_ref, rows_ref, ident_ref, tokens_ref, base_ref, own, arrived, *, exp_dev):
    tok_dev, half = base_ref.shape
    copy = pltpu.make_async_copy(
        tokens_ref.at[:, pl.ds(pl.multiple_of(group_ref[0] * half, half), half)], own, arrived
    )
    copy.start()
    copy.wait()
    for i, (near,) in mixed(rows_ref, tok_dev, exp_dev, (0,)):
        here = slice(i * BLOCK, (i + 1) * BLOCK)
        base_ref[:, here] = near + ident_ref[:, 0:1] * own[:, here]


def cost(offsets, tok_dev, rows, half):
    depth = rows.shape[0] * (rows.shape[1] * 128 // half)
    return pl.CostEstimate(
        flops=6 * offsets * tok_dev * depth * half, bytes_accessed=4 * depth * half, transcendentals=0
    )


def combine(rows, tok_dev, half, exp_dev):
    vmem = pl.BlockSpec(memory_space=pltpu.VMEM)
    return pl.pallas_call(
        functools.partial(combine_kernel, exp_dev=exp_dev),
        out_shape=[jax.ShapeDtypeStruct((tok_dev, half // 2), jnp.float32)] * 6,
        in_specs=[vmem],
        out_specs=[vmem] * 6,
        compiler_params=pltpu.CompilerParams(vmem_limit_bytes=MIX_VMEM),
        cost_estimate=cost(3, tok_dev, rows, half),
        name="combine",
    )(rows)


def own_sum(group, rows, ident, tokens, exp_dev):
    tok_dev, width = tokens.shape
    half = width // 2
    vmem = pl.BlockSpec(memory_space=pltpu.VMEM)
    return pl.pallas_call(
        functools.partial(own_kernel, exp_dev=exp_dev),
        out_shape=jax.ShapeDtypeStruct((tok_dev, half), jnp.float32),
        in_specs=[pl.BlockSpec(memory_space=pltpu.SMEM), vmem, vmem, pl.BlockSpec(memory_space=pl.ANY)],
        out_specs=vmem,
        scratch_shapes=[pltpu.VMEM((tok_dev, half), jnp.float32), pltpu.SemaphoreType.DMA],
        compiler_params=pltpu.CompilerParams(vmem_limit_bytes=MIX_VMEM),
        cost_estimate=cost(1, tok_dev, rows, half),
        name="own_sum",
    )(group, rows, ident, in_hbm(tokens))


def finish_kernel(base_ref, left_ref, more_left_ref, right_ref, more_right_ref, out_ref):
    _, cut = left_ref.shape
    out_ref[:, :cut] = base_ref[:, :cut] + more_left_ref[...] + left_ref[...]
    out_ref[:, cut:] = base_ref[:, cut:] + more_right_ref[...] + right_ref[...]


def finish(base, *parts):
    vmem = pl.BlockSpec(memory_space=pltpu.VMEM)
    return pl.pallas_call(
        finish_kernel,
        out_shape=jax.ShapeDtypeStruct(base.shape, jnp.float32),
        in_specs=[vmem] * 5,
        out_specs=vmem,
        compiler_params=pltpu.CompilerParams(vmem_limit_bytes=MIX_VMEM),
        name="finish",
    )(base, *parts)


def shift(count, by):
    return [(i, (i + by) % count) for i in range(count)]


def shards(tokens, route_ids, route_weights, expert_rows):
    group = lax.axis_index("grp")
    ep_count = lax.axis_size(EP)
    far = lax.axis_size("zh")
    low = lax.axis_size("zl")
    near = ep_count // far
    tok_dev, top = route_ids.shape
    exp_dev, capacity, width = expert_rows.shape
    half = width // 2
    held = 2 * exp_dev
    per_group = exp_dev * ep_count
    experts = 2 * per_group

    taken = lax.ppermute(expert_rows, "grp", [(0, 1), (1, 0)])

    group_word = group.astype(jnp.int32).reshape(1)
    asked, ident = ask(group_word, route_ids.T, route_weights.T, ep_count, exp_dev, per_group)
    chosen = lax.all_to_all(asked[:, None, :], EP, 0, 0, tiled=True).reshape(ep_count, 128)

    row = jnp.arange(ep_count * held, dtype=jnp.int32)[:, None]
    r_side = row // (ep_count * exp_dev)
    r_near = row % (ep_count * exp_dev) // (far * exp_dev)
    r_far = row % (far * exp_dev) // exp_dev
    r_exp = row % exp_dev
    zh = lax.axis_index("zh")
    home = (r_near // low * far + (zh + r_far) % far) * low + r_near % low
    lane = r_side * exp_dev + r_exp

    chosen, home, lane, taken = lax.optimization_barrier((chosen, home, lane, taken))
    outgoing = pick(group_word, chosen, home, lane, in_hbm(expert_rows), taken, near)

    rows = lax.all_to_all(outgoing, NEAR, 0, 0, tiled=True)
    up, down = shift(far, 1), shift(far, -1)
    far_up, far_down, near_left, near_right, prev_left, prev_right = combine(rows, tok_dev, half, exp_dev)
    far_up, far_down = lax.ppermute(far_up, "zh", up), lax.ppermute(far_down, "zh", down)
    more_right, more_left = lax.ppermute(near_right, "zh", up), lax.ppermute(prev_left, "zh", down)
    base = own_sum(group_word, rows, ident, tokens, exp_dev)
    left = lax.ppermute(near_left + far_up, "zh", up)
    right = lax.ppermute(prev_right + far_down, "zh", down)
    return finish(base, left, more_left, right, more_right)


def solution(mesh):
    torus = Mesh(mesh.devices.reshape(mesh.shape["grp"], 4, 4, 4, 2), ("grp",) + EP)
    in_specs = (P(EP, None), P(EP, None), P(EP, None), P(("grp",) + EP, None, None))
    return jax.shard_map(
        shards, mesh=torus, in_specs=in_specs, out_specs=P(EP, "grp"), check_vma=False
    )
```

```python
import functools

import jax
import jax.numpy as jnp
from jax import lax
from jax.sharding import Mesh
from jax.sharding import PartitionSpec as P
from jax.experimental import pallas as pl
from jax.experimental.pallas import tpu as pltpu

EP = ("x", "y", "zh", "zl")
NEAR = ("x", "y", "zl")
BLOCK = 768
PICK_BLOCK = 1536
PICK_VMEM = 24 * 1024 * 1024
MIX_VMEM = 24 * 1024 * 1024


def halves(x):
    high = x.astype(jnp.bfloat16)
    rest = x - high.astype(jnp.float32)
    middle = rest.astype(jnp.bfloat16)
    return high, middle, rest - middle.astype(jnp.float32)


def in_hbm(x):
    return pltpu.with_memory_space_constraint(x, pltpu.HBM)


def mul(a, b):
    return jnp.dot(a, b, preferred_element_type=jnp.float32)


def ask_kernel(
    group_ref, ids_hbm, weights_hbm, out_ref, ident_ref, ids_ref, weights_ref, both, arrived, *, exp_dev, per_group
):
    copies = [
        pltpu.make_async_copy(ids_hbm, ids_ref, arrived.at[0]),
        pltpu.make_async_copy(weights_hbm, weights_ref, arrived.at[1]),
    ]
    for copy in copies:
        copy.start()
    for copy in copies:
        copy.wait()
    top, count = ids_ref.shape
    chips = out_ref.shape[0]
    gap = 2 * exp_dev
    second = both.shape[0] // 2
    ids = ids_ref[...]
    chip = jnp.where(ids < 2 * per_group, lax.div(lax.rem(ids, per_group), exp_dev), -1)
    both[...] = jnp.zeros_like(both)
    both[0:top, :] = ids.astype(jnp.float32)
    both[second : second + top, :] = weights_ref[...]
    columns = both[...].T
    together = 128 // count
    chip_lines = lax.broadcasted_iota(jnp.int32, (chips, 128), 0)
    values = []
    lanes = lax.broadcasted_iota(jnp.int32, (count, 128), 1)
    token = (lax.broadcasted_iota(jnp.int32, (count, 128), 0) + 1).astype(jnp.float32)
    total = jnp.zeros((chips, 128), jnp.float32)
    ident = jnp.zeros((count, 1), jnp.float32)
    for k in range(top):
        names = columns[:, k : k + 1].astype(jnp.int32)
        ident += jnp.where(names < 2 * per_group, 0.0, columns[:, second + k : second + k + 1])
        place = jnp.where(lax.div(names, per_group) == group_ref[0], 0, exp_dev) + lax.rem(names, exp_dev)
        high, middle, low = halves(columns[:, second + k : second + k + 1])
        value = jnp.where(lanes == place, token, 0.0)
        value = jnp.where(lanes == place + gap, high.astype(jnp.float32), value)
        value = jnp.where(lanes == place + 2 * gap, middle.astype(jnp.float32), value)
        value = jnp.where(lanes == place + 3 * gap, low, value)
        values.append(value)
        if len(values) == together:
            names = jnp.concatenate([chip[j : j + 1, :] for j in range(k + 1 - together, k + 1)], axis=1)
            where = (chip_lines == names).astype(jnp.float32).astype(jnp.bfloat16)
            total += mul(where, jnp.concatenate(values, axis=0).astype(jnp.bfloat16))
            values = []
    ident_ref[...] = jnp.broadcast_to(ident, ident_ref.shape)
    weight = total + pltpu.roll(total, 128 - gap, 1) + pltpu.roll(total, 128 - 2 * gap, 1)
    lanes = lax.broadcasted_iota(jnp.int32, total.shape, 1)
    out_ref[...] = jnp.where(lanes < gap, total, jnp.where(lanes < 2 * gap, weight, 0.0))


def ask(group, ids, weights, chips, exp_dev, per_group):
    top, count = ids.shape
    vmem = pl.BlockSpec(memory_space=pltpu.VMEM)
    hbm = pl.BlockSpec(memory_space=pl.ANY)
    return pl.pallas_call(
        functools.partial(ask_kernel, exp_dev=exp_dev, per_group=per_group),
        out_shape=(
            jax.ShapeDtypeStruct((chips, 128), jnp.float32),
            jax.ShapeDtypeStruct((count, 128), jnp.float32),
        ),
        in_specs=[pl.BlockSpec(memory_space=pltpu.SMEM), hbm, hbm],
        out_specs=(vmem, vmem),
        scratch_shapes=[
            pltpu.VMEM((top, count), jnp.int32),
            pltpu.VMEM((top, count), jnp.float32),
            pltpu.VMEM((2 * (-(-top // 8) * 8), count), jnp.float32),
            pltpu.SemaphoreType.DMA((2,)),
        ],
        compiler_params=pltpu.CompilerParams(vmem_limit_bytes=MIX_VMEM),
        name="ask",
    )(group, in_hbm(ids), in_hbm(weights))


def pick_kernel(group_ref, chosen_ref, home_ref, lane_ref, own_ref, taken_ref, out_ref, held, arrived):
    sides, steps, exp_dev, capacity, block = held.shape
    start = pl.multiple_of(group_ref[0] * steps * block, block)
    copies = {}
    for i in range(steps):
        for side, ref in enumerate((own_ref, taken_ref)):
            copies[i, side] = pltpu.make_async_copy(
                ref.at[:, :, pl.ds(start + i * block, block)], held.at[side, i], arrived.at[side, i]
            )
            copies[i, side].start()

    chosen = chosen_ref[...]
    count = home_ref.shape[0]
    gap = sides * exp_dev
    homes = lax.broadcasted_iota(jnp.int32, (count, chosen.shape[0]), 1)
    earlier = (homes < home_ref[...]).astype(jnp.float32).astype(jnp.bfloat16)
    before = mul(earlier, (chosen > 0).astype(jnp.float32).astype(jnp.bfloat16))
    high, middle, low = halves(chosen)
    home_lanes = lax.broadcasted_iota(jnp.int32, chosen.shape, 1)
    packed = jnp.where(home_lanes < 4 * gap, pltpu.roll(middle.astype(jnp.float32), 2 * gap, 1), pltpu.roll(low, 4 * gap, 1))
    packed = jnp.where(home_lanes < 2 * gap, high.astype(jnp.float32), packed)
    this = (homes == home_ref[...]).astype(jnp.float32).astype(jnp.bfloat16)
    here = mul(this, packed.astype(jnp.bfloat16))
    lanes = lax.broadcasted_iota(jnp.int32, here.shape, 1)
    mine = lanes == lane_ref[...]
    token = jnp.sum(jnp.where(mine, here, 0.0), axis=1, keepdims=True)
    parts = (lax.rem(lanes, 2 * gap) == lane_ref[...] + gap) & (lanes < 6 * gap)
    weight = jnp.sum(jnp.where(parts, here, 0.0), axis=1, keepdims=True)
    rank = jnp.sum(jnp.where(mine, before, 0.0), axis=1, keepdims=True)
    code = jnp.where(token > 0, rank.astype(jnp.int32) + capacity * lax.rem(lane_ref[...], exp_dev), -1)
    slot = lax.broadcasted_iota(jnp.int32, (count, exp_dev * capacity), 1)
    select = (code == slot).astype(jnp.float32).astype(jnp.bfloat16)

    targets, lines, group = out_ref.shape
    each = count // sides
    rows = each // targets
    lanes = lanes[:each]
    note = jnp.where(lanes == 0, token[:each], jnp.where(lanes == 1, weight[:each], 0.0))
    note = jnp.where(lanes == 2, token[each:], jnp.where(lanes == 3, weight[each:], note))
    out_ref[:, lines - rows :, :] = note.reshape(targets, rows, group)
    per = block // group
    for i in range(steps):
        for side in range(sides):
            copies[i, side].wait()
            high, middle, _ = halves(held[side, i].reshape(exp_dev * capacity, block))
            wanted = select[side * each : (side + 1) * each, :]
            value = mul(wanted, high) + mul(wanted, middle)
            for j in range(per):
                line = ((i * per + j) * sides + side) * rows
                out_ref[:, line : line + rows, :] = value[:, j * group : (j + 1) * group].reshape(targets, rows, group)


def pick(group, chosen, home, lane, own, taken, targets):
    exp_dev, capacity, width = own.shape
    half = width // 2
    steps = half // PICK_BLOCK
    count = home.shape[0]
    slots = exp_dev * capacity
    lines = count // targets * half // 128 + count // targets // 2
    vmem = pl.BlockSpec(memory_space=pltpu.VMEM)
    hbm = pl.BlockSpec(memory_space=pl.ANY)
    return pl.pallas_call(
        pick_kernel,
        out_shape=jax.ShapeDtypeStruct((targets, lines, 128), jnp.float32),
        in_specs=[pl.BlockSpec(memory_space=pltpu.SMEM), vmem, vmem, vmem, hbm, hbm],
        out_specs=vmem,
        scratch_shapes=[
            pltpu.VMEM((2, steps, exp_dev, capacity, PICK_BLOCK), jnp.float32),
            pltpu.SemaphoreType.DMA((2, steps)),
        ],
        compiler_params=pltpu.CompilerParams(vmem_limit_bytes=PICK_VMEM),
        cost_estimate=pl.CostEstimate(
            flops=4 * count * slots * half, bytes_accessed=4 * (2 * slots + count) * half, transcendentals=0
        ),
        name="pick",
    )(group, chosen, home, lane, own, taken)


def mixed(rows_ref, tok_dev, exp_dev, offsets):
    far = 4
    sources, lines, group = rows_ref.shape
    rows = far * exp_dev
    count = len(offsets) * tok_dev
    note = rows_ref[:, lines - rows :, :].reshape(sources * rows, group)
    line = lax.broadcasted_iota(jnp.int32, (sources * rows, count), 0)
    out_line = lax.broadcasted_iota(jnp.int32, (sources * rows, count), 1)
    fits = lax.div(lax.rem(line, rows), exp_dev) == lax.div(out_line, tok_dev) + offsets[0]
    token = jnp.where(fits, lax.rem(out_line, tok_dev) + 1, -1).astype(jnp.float32)
    sides = []
    for side in range(2):
        named = note[:, 2 * side : 2 * side + 1] == token
        mix = jnp.where(named, note[:, 2 * side + 1 : 2 * side + 2], 0.0)
        sides.append(mix.reshape(sources, rows, count))
    mix = jnp.concatenate(sides, axis=1).reshape(2 * sources * rows, count).T
    m_high, m_middle, _ = halves(mix)
    both = jnp.concatenate([m_high, m_middle], axis=0)
    per = BLOCK // group
    for i in range((lines - rows) // (2 * rows * per)):
        parts = [rows_ref[:, 2 * rows * (i * per + j) : 2 * rows * (i * per + j + 1), :] for j in range(per)]
        block = jnp.concatenate([part.reshape(2 * sources * rows, group) for part in parts], axis=1)
        high, middle, _ = halves(block)
        value = mul(both, high)
        value = value[:count] + (value[count:] + mul(m_high, middle))
        yield i, [value[o * tok_dev : (o + 1) * tok_dev] for o in range(len(offsets))]


def combine_kernel(rows_ref, far_up, far_down, near_left, near_right, prev_left, prev_right, *, exp_dev):
    tok_dev, cut = far_up.shape
    for i, (nxt, opposite, prev) in mixed(rows_ref, tok_dev, exp_dev, (1, 2, 3)):
        first = i * BLOCK < cut
        here = slice(i * BLOCK % cut, i * BLOCK % cut + BLOCK)
        (far_up if first else far_down)[:, here] = opposite
        (near_left if first else near_right)[:, here] = nxt
        (prev_left if first else prev_right)[:, here] = prev


def own_kernel(group_ref, rows_ref, ident_ref, tokens_ref, base_ref, own, arrived, *, exp_dev):
    tok_dev, half = base_ref.shape
    copy = pltpu.make_async_copy(
        tokens_ref.at[:, pl.ds(pl.multiple_of(group_ref[0] * half, half), half)], own, arrived
    )
    copy.start()
    copy.wait()
    for i, (near,) in mixed(rows_ref, tok_dev, exp_dev, (0,)):
        here = slice(i * BLOCK, (i + 1) * BLOCK)
        base_ref[:, here] = near + ident_ref[:, 0:1] * own[:, here]


def cost(offsets, tok_dev, rows, half):
    depth = rows.shape[0] * (rows.shape[1] * 128 // half)
    return pl.CostEstimate(
        flops=6 * offsets * tok_dev * depth * half, bytes_accessed=4 * depth * half, transcendentals=0
    )


def combine(rows, tok_dev, half, exp_dev):
    vmem = pl.BlockSpec(memory_space=pltpu.VMEM)
    return pl.pallas_call(
        functools.partial(combine_kernel, exp_dev=exp_dev),
        out_shape=[jax.ShapeDtypeStruct((tok_dev, half // 2), jnp.float32)] * 6,
        in_specs=[vmem],
        out_specs=[vmem] * 6,
        compiler_params=pltpu.CompilerParams(vmem_limit_bytes=MIX_VMEM),
        cost_estimate=cost(3, tok_dev, rows, half),
        name="combine",
    )(rows)


def own_sum(group, rows, ident, tokens, exp_dev):
    tok_dev, width = tokens.shape
    half = width // 2
    vmem = pl.BlockSpec(memory_space=pltpu.VMEM)
    return pl.pallas_call(
        functools.partial(own_kernel, exp_dev=exp_dev),
        out_shape=jax.ShapeDtypeStruct((tok_dev, half), jnp.float32),
        in_specs=[pl.BlockSpec(memory_space=pltpu.SMEM), vmem, vmem, pl.BlockSpec(memory_space=pl.ANY)],
        out_specs=vmem,
        scratch_shapes=[pltpu.VMEM((tok_dev, half), jnp.float32), pltpu.SemaphoreType.DMA],
        compiler_params=pltpu.CompilerParams(vmem_limit_bytes=MIX_VMEM),
        cost_estimate=cost(1, tok_dev, rows, half),
        name="own_sum",
    )(group, rows, ident, in_hbm(tokens))


def finish_kernel(base_ref, left_ref, more_left_ref, right_ref, more_right_ref, out_ref):
    _, cut = left_ref.shape
    out_ref[:, :cut] = base_ref[:, :cut] + more_left_ref[...] + left_ref[...]
    out_ref[:, cut:] = base_ref[:, cut:] + more_right_ref[...] + right_ref[...]


def finish(base, *parts):
    vmem = pl.BlockSpec(memory_space=pltpu.VMEM)
    return pl.pallas_call(
        finish_kernel,
        out_shape=jax.ShapeDtypeStruct(base.shape, jnp.float32),
        in_specs=[vmem] * 5,
        out_specs=vmem,
        compiler_params=pltpu.CompilerParams(vmem_limit_bytes=MIX_VMEM),
        name="finish",
    )(base, *parts)


def shift(count, by):
    return [(i, (i + by) % count) for i in range(count)]


def shards(tokens, route_ids, route_weights, expert_rows):
    group = lax.axis_index("grp")
    ep_count = lax.axis_size(EP)
    far = lax.axis_size("zh")
    low = lax.axis_size("zl")
    near = ep_count // far
    tok_dev, top = route_ids.shape
    exp_dev, capacity, width = expert_rows.shape
    half = width // 2
    held = 2 * exp_dev
    per_group = exp_dev * ep_count
    experts = 2 * per_group

    taken = lax.ppermute(expert_rows, "grp", [(0, 1), (1, 0)])

    group_word = group.astype(jnp.int32).reshape(1)
    asked, ident = ask(group_word, route_ids.T, route_weights.T, ep_count, exp_dev, per_group)
    chosen = lax.all_to_all(asked[:, None, :], EP, 0, 0, tiled=True).reshape(ep_count, 128)

    row = jnp.arange(ep_count * held, dtype=jnp.int32)[:, None]
    r_side = row // (ep_count * exp_dev)
    r_near = row % (ep_count * exp_dev) // (far * exp_dev)
    r_far = row % (far * exp_dev) // exp_dev
    r_exp = row % exp_dev
    zh = lax.axis_index("zh")
    home = (r_near // low * far + (zh + r_far) % far) * low + r_near % low
    lane = r_side * exp_dev + r_exp

    chosen, home, lane, taken = lax.optimization_barrier((chosen, home, lane, taken))
    outgoing = pick(group_word, chosen, home, lane, in_hbm(expert_rows), taken, near)

    rows = lax.all_to_all(outgoing, NEAR, 0, 0, tiled=True)
    up, down = shift(far, 1), shift(far, -1)
    far_up, far_down, near_left, near_right, prev_left, prev_right = combine(rows, tok_dev, half, exp_dev)
    far_up, far_down = lax.ppermute(far_up, "zh", up), lax.ppermute(far_down, "zh", down)
    more_right, more_left = lax.ppermute(near_right, "zh", up), lax.ppermute(prev_left, "zh", down)
    base = own_sum(group_word, rows, ident, tokens, exp_dev)
    left = lax.ppermute(near_left + far_up, "zh", up)
    right = lax.ppermute(prev_right + far_down, "zh", down)
    return finish(base, left, more_left, right, more_right)


def solution(mesh):
    torus = Mesh(mesh.devices.reshape(mesh.shape["grp"], 4, 4, 4, 2), ("grp",) + EP)
    in_specs = (P(EP, None), P(EP, None), P(EP, None), P(("grp",) + EP, None, None))
    return jax.shard_map(
        shards, mesh=torus, in_specs=in_specs, out_specs=P(EP, "grp"), check_vma=False
    )
```

```python
import functools

import jax
import jax.numpy as jnp
from jax import lax
from jax.sharding import Mesh
from jax.sharding import PartitionSpec as P
from jax.experimental import pallas as pl
from jax.experimental.pallas import tpu as pltpu

EP = ("x", "y", "zh", "zl")
NEAR = ("x", "y", "zl")
BLOCK = 1536
PICK_BLOCK = 1536
PICK_VMEM = 24 * 1024 * 1024
MIX_VMEM = 24 * 1024 * 1024


def halves(x):
    high = x.astype(jnp.bfloat16)
    rest = x - high.astype(jnp.float32)
    middle = rest.astype(jnp.bfloat16)
    return high, middle, rest - middle.astype(jnp.float32)


def in_hbm(x):
    return pltpu.with_memory_space_constraint(x, pltpu.HBM)


def mul(a, b):
    return jnp.dot(a, b, preferred_element_type=jnp.float32)


def ask_kernel(
    group_ref, ids_hbm, weights_hbm, out_ref, ident_ref, ids_ref, weights_ref, both, arrived, *, exp_dev, per_group
):
    copies = [
        pltpu.make_async_copy(ids_hbm, ids_ref, arrived.at[0]),
        pltpu.make_async_copy(weights_hbm, weights_ref, arrived.at[1]),
    ]
    for copy in copies:
        copy.start()
    for copy in copies:
        copy.wait()
    top, count = ids_ref.shape
    chips = out_ref.shape[0]
    gap = 2 * exp_dev
    second = both.shape[0] // 2
    ids = ids_ref[...]
    chip = jnp.where(ids < 2 * per_group, lax.div(lax.rem(ids, per_group), exp_dev), -1)
    both[...] = jnp.zeros_like(both)
    both[0:top, :] = ids.astype(jnp.float32)
    both[second : second + top, :] = weights_ref[...]
    columns = both[...].T
    together = 128 // count
    chip_lines = lax.broadcasted_iota(jnp.int32, (chips, 128), 0)
    values = []
    lanes = lax.broadcasted_iota(jnp.int32, (count, 128), 1)
    token = (lax.broadcasted_iota(jnp.int32, (count, 128), 0) + 1).astype(jnp.float32)
    total = jnp.zeros((chips, 128), jnp.float32)
    ident = jnp.zeros((count, 1), jnp.float32)
    for k in range(top):
        names = columns[:, k : k + 1].astype(jnp.int32)
        ident += jnp.where(names < 2 * per_group, 0.0, columns[:, second + k : second + k + 1])
        place = jnp.where(lax.div(names, per_group) == group_ref[0], 0, exp_dev) + lax.rem(names, exp_dev)
        high, middle, low = halves(columns[:, second + k : second + k + 1])
        value = jnp.where(lanes == place, token, 0.0)
        value = jnp.where(lanes == place + gap, high.astype(jnp.float32), value)
        value = jnp.where(lanes == place + 2 * gap, middle.astype(jnp.float32), value)
        value = jnp.where(lanes == place + 3 * gap, low, value)
        values.append(value)
        if len(values) == together:
            names = jnp.concatenate([chip[j : j + 1, :] for j in range(k + 1 - together, k + 1)], axis=1)
            where = (chip_lines == names).astype(jnp.float32).astype(jnp.bfloat16)
            total += mul(where, jnp.concatenate(values, axis=0).astype(jnp.bfloat16))
            values = []
    ident_ref[...] = jnp.broadcast_to(ident, ident_ref.shape)
    weight = total + pltpu.roll(total, 128 - gap, 1) + pltpu.roll(total, 128 - 2 * gap, 1)
    lanes = lax.broadcasted_iota(jnp.int32, total.shape, 1)
    out_ref[...] = jnp.where(lanes < gap, total, jnp.where(lanes < 2 * gap, weight, 0.0))


def ask(group, ids, weights, chips, exp_dev, per_group):
    top, count = ids.shape
    vmem = pl.BlockSpec(memory_space=pltpu.VMEM)
    hbm = pl.BlockSpec(memory_space=pl.ANY)
    return pl.pallas_call(
        functools.partial(ask_kernel, exp_dev=exp_dev, per_group=per_group),
        out_shape=(
            jax.ShapeDtypeStruct((chips, 128), jnp.float32),
            jax.ShapeDtypeStruct((count, 128), jnp.float32),
        ),
        in_specs=[pl.BlockSpec(memory_space=pltpu.SMEM), hbm, hbm],
        out_specs=(vmem, vmem),
        scratch_shapes=[
            pltpu.VMEM((top, count), jnp.int32),
            pltpu.VMEM((top, count), jnp.float32),
            pltpu.VMEM((2 * (-(-top // 8) * 8), count), jnp.float32),
            pltpu.SemaphoreType.DMA((2,)),
        ],
        compiler_params=pltpu.CompilerParams(vmem_limit_bytes=MIX_VMEM),
        name="ask",
    )(group, in_hbm(ids), in_hbm(weights))


def pick_kernel(group_ref, chosen_ref, home_ref, lane_ref, own_ref, taken_ref, out_ref, held, arrived):
    sides, steps, exp_dev, capacity, block = held.shape
    start = pl.multiple_of(group_ref[0] * steps * block, block)
    copies = {}
    for i in range(steps):
        for side, ref in enumerate((own_ref, taken_ref)):
            copies[i, side] = pltpu.make_async_copy(
                ref.at[:, :, pl.ds(start + i * block, block)], held.at[side, i], arrived.at[side, i]
            )
            copies[i, side].start()

    chosen = chosen_ref[...]
    count = home_ref.shape[0]
    gap = sides * exp_dev
    homes = lax.broadcasted_iota(jnp.int32, (count, chosen.shape[0]), 1)
    earlier = (homes < home_ref[...]).astype(jnp.float32).astype(jnp.bfloat16)
    before = mul(earlier, (chosen > 0).astype(jnp.float32).astype(jnp.bfloat16))
    high, middle, low = halves(chosen)
    home_lanes = lax.broadcasted_iota(jnp.int32, chosen.shape, 1)
    packed = jnp.where(home_lanes < 4 * gap, pltpu.roll(middle.astype(jnp.float32), 2 * gap, 1), pltpu.roll(low, 4 * gap, 1))
    packed = jnp.where(home_lanes < 2 * gap, high.astype(jnp.float32), packed)
    this = (homes == home_ref[...]).astype(jnp.float32).astype(jnp.bfloat16)
    here = mul(this, packed.astype(jnp.bfloat16))
    lanes = lax.broadcasted_iota(jnp.int32, here.shape, 1)
    mine = lanes == lane_ref[...]
    token = jnp.sum(jnp.where(mine, here, 0.0), axis=1, keepdims=True)
    parts = (lax.rem(lanes, 2 * gap) == lane_ref[...] + gap) & (lanes < 6 * gap)
    weight = jnp.sum(jnp.where(parts, here, 0.0), axis=1, keepdims=True)
    rank = jnp.sum(jnp.where(mine, before, 0.0), axis=1, keepdims=True)
    code = jnp.where(token > 0, rank.astype(jnp.int32) + capacity * lax.rem(lane_ref[...], exp_dev), -1)
    slot = lax.broadcasted_iota(jnp.int32, (count, exp_dev * capacity), 1)
    select = (code == slot).astype(jnp.float32).astype(jnp.bfloat16)

    targets, lines, group = out_ref.shape
    each = count // sides
    rows = each // targets
    lanes = lanes[:each]
    note = jnp.where(lanes == 0, token[:each], jnp.where(lanes == 1, weight[:each], 0.0))
    note = jnp.where(lanes == 2, token[each:], jnp.where(lanes == 3, weight[each:], note))
    out_ref[:, lines - rows :, :] = note.reshape(targets, rows, group)
    per = block // group
    for i in range(steps):
        for side in range(sides):
            copies[i, side].wait()
            high, middle, _ = halves(held[side, i].reshape(exp_dev * capacity, block))
            wanted = select[side * each : (side + 1) * each, :]
            value = mul(wanted, high) + mul(wanted, middle)
            for j in range(per):
                line = ((i * per + j) * sides + side) * rows
                out_ref[:, line : line + rows, :] = value[:, j * group : (j + 1) * group].reshape(targets, rows, group)


def pick(group, chosen, home, lane, own, taken, targets):
    exp_dev, capacity, width = own.shape
    half = width // 2
    steps = half // PICK_BLOCK
    count = home.shape[0]
    slots = exp_dev * capacity
    lines = count // targets * half // 128 + count // targets // 2
    vmem = pl.BlockSpec(memory_space=pltpu.VMEM)
    hbm = pl.BlockSpec(memory_space=pl.ANY)
    return pl.pallas_call(
        pick_kernel,
        out_shape=jax.ShapeDtypeStruct((targets, lines, 128), jnp.float32),
        in_specs=[pl.BlockSpec(memory_space=pltpu.SMEM), vmem, vmem, vmem, hbm, hbm],
        out_specs=vmem,
        scratch_shapes=[
            pltpu.VMEM((2, steps, exp_dev, capacity, PICK_BLOCK), jnp.float32),
            pltpu.SemaphoreType.DMA((2, steps)),
        ],
        compiler_params=pltpu.CompilerParams(vmem_limit_bytes=PICK_VMEM),
        cost_estimate=pl.CostEstimate(
            flops=4 * count * slots * half, bytes_accessed=4 * (2 * slots + count) * half, transcendentals=0
        ),
        name="pick",
    )(group, chosen, home, lane, own, taken)


def mixed(rows_ref, tok_dev, exp_dev, offsets):
    far = 4
    sources, lines, group = rows_ref.shape
    rows = far * exp_dev
    count = len(offsets) * tok_dev
    note = rows_ref[:, lines - rows :, :].reshape(sources * rows, group)
    line = lax.broadcasted_iota(jnp.int32, (sources * rows, count), 0)
    out_line = lax.broadcasted_iota(jnp.int32, (sources * rows, count), 1)
    fits = lax.div(lax.rem(line, rows), exp_dev) == lax.div(out_line, tok_dev) + offsets[0]
    token = jnp.where(fits, lax.rem(out_line, tok_dev) + 1, -1).astype(jnp.float32)
    sides = []
    for side in range(2):
        named = note[:, 2 * side : 2 * side + 1] == token
        mix = jnp.where(named, note[:, 2 * side + 1 : 2 * side + 2], 0.0)
        sides.append(mix.reshape(sources, rows, count))
    mix = jnp.concatenate(sides, axis=1).reshape(2 * sources * rows, count).T
    m_high, m_middle, _ = halves(mix)
    both = jnp.concatenate([m_high, m_middle], axis=0)
    per = BLOCK // group
    for i in range((lines - rows) // (2 * rows * per)):
        parts = [rows_ref[:, 2 * rows * (i * per + j) : 2 * rows * (i * per + j + 1), :] for j in range(per)]
        block = jnp.concatenate([part.reshape(2 * sources * rows, group) for part in parts], axis=1)
        high, middle, _ = halves(block)
        value = mul(both, high)
        value = value[:count] + (value[count:] + mul(m_high, middle))
        yield i, [value[o * tok_dev : (o + 1) * tok_dev] for o in range(len(offsets))]


def combine_kernel(rows_ref, far_up, far_down, near_left, near_right, prev_left, prev_right, *, exp_dev):
    tok_dev, cut = far_up.shape
    for i, (nxt, opposite, prev) in mixed(rows_ref, tok_dev, exp_dev, (1, 2, 3)):
        first = i * BLOCK < cut
        here = slice(i * BLOCK % cut, i * BLOCK % cut + BLOCK)
        (far_up if first else far_down)[:, here] = opposite
        (near_left if first else near_right)[:, here] = nxt
        (prev_left if first else prev_right)[:, here] = prev


def own_kernel(group_ref, rows_ref, ident_ref, tokens_ref, base_ref, own, arrived, *, exp_dev):
    tok_dev, half = base_ref.shape
    copy = pltpu.make_async_copy(
        tokens_ref.at[:, pl.ds(pl.multiple_of(group_ref[0] * half, half), half)], own, arrived
    )
    copy.start()
    copy.wait()
    for i, (near,) in mixed(rows_ref, tok_dev, exp_dev, (0,)):
        here = slice(i * BLOCK, (i + 1) * BLOCK)
        base_ref[:, here] = near + ident_ref[:, 0:1] * own[:, here]


def cost(offsets, tok_dev, rows, half):
    depth = rows.shape[0] * (rows.shape[1] * 128 // half)
    return pl.CostEstimate(
        flops=6 * offsets * tok_dev * depth * half, bytes_accessed=4 * depth * half, transcendentals=0
    )


def combine(rows, tok_dev, half, exp_dev):
    vmem = pl.BlockSpec(memory_space=pltpu.VMEM)
    return pl.pallas_call(
        functools.partial(combine_kernel, exp_dev=exp_dev),
        out_shape=[jax.ShapeDtypeStruct((tok_dev, half // 2), jnp.float32)] * 6,
        in_specs=[vmem],
        out_specs=[vmem] * 6,
        compiler_params=pltpu.CompilerParams(vmem_limit_bytes=MIX_VMEM),
        cost_estimate=cost(3, tok_dev, rows, half),
        name="combine",
    )(rows)


def own_sum(group, rows, ident, tokens, exp_dev):
    tok_dev, width = tokens.shape
    half = width // 2
    vmem = pl.BlockSpec(memory_space=pltpu.VMEM)
    return pl.pallas_call(
        functools.partial(own_kernel, exp_dev=exp_dev),
        out_shape=jax.ShapeDtypeStruct((tok_dev, half), jnp.float32),
        in_specs=[pl.BlockSpec(memory_space=pltpu.SMEM), vmem, vmem, pl.BlockSpec(memory_space=pl.ANY)],
        out_specs=vmem,
        scratch_shapes=[pltpu.VMEM((tok_dev, half), jnp.float32), pltpu.SemaphoreType.DMA],
        compiler_params=pltpu.CompilerParams(vmem_limit_bytes=MIX_VMEM),
        cost_estimate=cost(1, tok_dev, rows, half),
        name="own_sum",
    )(group, rows, ident, in_hbm(tokens))


def finish_kernel(base_ref, left_ref, more_left_ref, right_ref, more_right_ref, out_ref):
    _, cut = left_ref.shape
    out_ref[:, :cut] = base_ref[:, :cut] + more_left_ref[...] + left_ref[...]
    out_ref[:, cut:] = base_ref[:, cut:] + more_right_ref[...] + right_ref[...]


def finish(base, *parts):
    vmem = pl.BlockSpec(memory_space=pltpu.VMEM)
    return pl.pallas_call(
        finish_kernel,
        out_shape=jax.ShapeDtypeStruct(base.shape, jnp.float32),
        in_specs=[vmem] * 5,
        out_specs=vmem,
        compiler_params=pltpu.CompilerParams(vmem_limit_bytes=MIX_VMEM),
        name="finish",
    )(base, *parts)


def shift(count, by):
    return [(i, (i + by) % count) for i in range(count)]


def shards(tokens, route_ids, route_weights, expert_rows):
    group = lax.axis_index("grp")
    ep_count = lax.axis_size(EP)
    far = lax.axis_size("zh")
    low = lax.axis_size("zl")
    near = ep_count // far
    tok_dev, top = route_ids.shape
    exp_dev, capacity, width = expert_rows.shape
    half = width // 2
    held = 2 * exp_dev
    per_group = exp_dev * ep_count
    experts = 2 * per_group

    taken = lax.ppermute(expert_rows, "grp", [(0, 1), (1, 0)])

    group_word = group.astype(jnp.int32).reshape(1)
    asked, ident = ask(group_word, route_ids.T, route_weights.T, ep_count, exp_dev, per_group)
    chosen = lax.all_to_all(asked[:, None, :], EP, 0, 0, tiled=True).reshape(ep_count, 128)

    row = jnp.arange(ep_count * held, dtype=jnp.int32)[:, None]
    r_side = row // (ep_count * exp_dev)
    r_near = row % (ep_count * exp_dev) // (far * exp_dev)
    r_far = row % (far * exp_dev) // exp_dev
    r_exp = row % exp_dev
    zh = lax.axis_index("zh")
    home = (r_near // low * far + (zh + r_far) % far) * low + r_near % low
    lane = r_side * exp_dev + r_exp

    chosen, home, lane, taken = lax.optimization_barrier((chosen, home, lane, taken))
    outgoing = pick(group_word, chosen, home, lane, in_hbm(expert_rows), taken, near)

    rows = lax.all_to_all(outgoing, NEAR, 0, 0, tiled=True)
    up, down = shift(far, 1), shift(far, -1)
    far_up, far_down, near_left, near_right, prev_left, prev_right = combine(rows, tok_dev, half, exp_dev)
    far_up, far_down = lax.ppermute(far_up, "zh", up), lax.ppermute(far_down, "zh", down)
    more_right, more_left = lax.ppermute(near_right, "zh", up), lax.ppermute(prev_left, "zh", down)
    base = own_sum(group_word, rows, ident, tokens, exp_dev)
    left = lax.ppermute(near_left + far_up, "zh", up)
    right = lax.ppermute(prev_right + far_down, "zh", down)
    return finish(base, left, more_left, right, more_right)


def solution(mesh):
    torus = Mesh(mesh.devices.reshape(mesh.shape["grp"], 4, 4, 4, 2), ("grp",) + EP)
    in_specs = (P(EP, None), P(EP, None), P(EP, None), P(("grp",) + EP, None, None))
    return jax.shard_map(
        shards, mesh=torus, in_specs=in_specs, out_specs=P(EP, "grp"), check_vma=False
    )
```
